128 devices in a mesh: wide: 8 (over y, core), grp: 16 (over z, x).
Axes of the slice: x: 4, y: 4, z: 4, core: 2. Of those that a mesh axis runs over, the one named last changes fastest.
Arguments:
- integrals: float32 [1200, 64, 1200], P('grp', 'wide'), may hold values from -6 to 6
- coeffs: float32 [1200, 800], replicated, may hold values from -0.1875 to 0.1875
Outputs:
- slab: float32 [800, 800, 64], P('grp', 'wide')
The draws below stay inside these ranges and needn't reach their ends.
All inputs are finite; a program needn't handle non-finite values.
Results may differ from the reference program's by a relative error of at most 0.00007.
Values sent between devices are 32-bit elements; how exact they have to be, the bound alone decides.
A program may use at most 128 MiB of HBM per device.

```python
import jax
import jax.numpy as jnp
from jax import lax

NAO = 1200
NMO = 800
PAIRS = 64


def block_levels(own_key, shape, split, smallest, top_value):
    def one(position, parts):
        draws = jax.random.uniform(jax.random.fold_in(jax.random.fold_in(own_key, 6), position), (parts,), jnp.float32, smallest / len(split), top_value / len(split))
        return jnp.repeat(jnp.exp(draws), shape[position] // parts).reshape((-1,) + (1,) * (len(shape) - position - 1))

    level = one(*split[0])
    for cut in split[1:]:
        level = level * one(*cut)
    return level


def normal_values(rng, dims, scale, limit, split=(), kind=jnp.bfloat16):
    entries = scale * jax.random.normal(rng, dims, jnp.float32)
    if split:
        entries = entries * block_levels(rng, dims, split, -0.22, 0.18)
    return jnp.clip(entries, -limit, limit).astype(kind)


def setup_inputs(seed: int = 0) -> dict:
    streams_of = jax.random.split(jax.random.key(seed), 3)
    return {
        "integrals": normal_values(streams_of[0], (NAO, PAIRS, NAO), 1.0, 6.0, ((0, 16), (1, 8)), jnp.float32),
        "coeffs": normal_values(streams_of[1], (NAO, NMO), NAO ** -0.5, 0.1875, (), jnp.float32),
    }


def reference(integrals, coeffs):
    basis = jnp.arange(NAO, dtype=jnp.int32)
    lower_mask = basis[None, :] <= basis[:, None]

    def one_pair(pair_index):
        matrix = lax.dynamic_index_in_dim(integrals, pair_index, 1, keepdims=False)
        symmetric = jnp.where(lower_mask, matrix, matrix.T)
        half_done = jnp.dot(symmetric, coeffs, precision=lax.Precision.HIGHEST)
        return jnp.dot(half_done.T, coeffs, precision=lax.Precision.HIGHEST)

    stacked = lax.map(one_pair, jnp.arange(PAIRS, dtype=jnp.int32))
    return jnp.transpose(stacked, (1, 2, 0))
```

```python
import functools

import jax
import jax.numpy as jnp
from jax import lax
from jax.experimental import pallas as pl
from jax.experimental.pallas import tpu as pltpu
from jax.sharding import PartitionSpec as P

MESH = pl.DeviceIdType.MESH
F32 = jnp.float32
BF16 = jnp.bfloat16
NT = (((1,), (1,)), ((), ()))
NN = (((1,), (0,)), ((), ()))

ROWS = 75
BAND = 80
OWN = 8
NAO = 1200
DEPTH = 1280
COLS = 100
KROWS = 50
SLOT = 56
PAIRS = 64


def split(v):
    hi = v.astype(BF16)
    return hi, (v - hi.astype(F32)).astype(BF16)


def widen(v):
    return jnp.concatenate([v, jnp.zeros((v.shape[0], DEPTH - NAO), F32)], axis=1)


def dot3(ah, al, bh, bl, dims):
    dot = functools.partial(lax.dot_general, dimension_numbers=dims, preferred_element_type=F32)
    return dot(ah, bh) + (dot(ah, bl) + dot(al, bh))


def kernel(x_ref, ct_ref, out_ref, xbuf, cbuf, th, tl, ch, cl, sent, got, ah, al, m, xr, n_, o,
           xsem, csem, s1, r1, l1, sx, rx, s2, r2, l2):
    g = lax.axis_index("grp")
    w = lax.axis_index("wide")
    y, c = w // 2, lax.rem(w, 2)
    other = 1 - c
    barrier = pltpu.get_barrier_semaphore()

    loads = [pltpu.make_async_copy(ct_ref, cbuf.at[pl.ds(0, 800), :], csem)]
    for p in range(OWN):
        loads.append(pltpu.make_async_copy(x_ref.at[:, p, :], xbuf.at[p], xsem.at[p]))
    for load in loads:
        load.start()

    src1 = g // 8
    src2 = y // 2

    def greet1(d, carry):
        gs = lax.rem(g + d, 16)

        @pl.when((d != 0) | (src1 != c))
        def _():
            pl.semaphore_signal(barrier, inc=1, device_id=(y * 2 + src1, gs), device_id_type=MESH)
        return carry

    lax.fori_loop(0, 16, greet1, 0)
    pl.semaphore_signal(barrier, inc=1, device_id=(y * 2 + other, g), device_id_type=MESH)

    def greet2(d, carry):
        gs = lax.rem(g + d // 4, 16)
        ws = lax.rem(y + lax.rem(d, 4), 4) * 2 + src2

        @pl.when((gs != g) | (ws != w))
        def _():
            pl.semaphore_signal(barrier, inc=1, device_id=(ws, gs), device_id_type=MESH)
        return carry

    lax.fori_loop(0, 64, greet2, 0)

    loads[0].wait()
    lane = lax.broadcasted_iota(jnp.int32, (16, DEPTH), 1)
    row = lax.broadcasted_iota(jnp.int32, (16, DEPTH), 0)
    for v in range(8):
        for b in range(7):
            value = widen(cbuf[pl.ds(COLS * v + 16 * b, 16), :])
            keep = lane < NAO
            if b == 6:
                keep = keep & (row < COLS - 96)
            hi, lo = split(jnp.where(keep, value, 0.0))
            ch[pl.ds(128 * v + 16 * b, 16), :] = hi
            cl[pl.ds(128 * v + 16 * b, 16), :] = lo
        ch[pl.ds(128 * v + 112, 16), :] = jnp.zeros((16, DEPTH), BF16)
        cl[pl.ds(128 * v + 112, 16), :] = jnp.zeros((16, DEPTH), BF16)

    for p in range(OWN):
        loads[1 + p].wait()
        for b in range(5):
            height = min(16, ROWS - 16 * b)
            value = widen(xbuf[p, pl.ds(16 * b, height), :])
            if height < 16:
                value = jnp.concatenate([value, jnp.zeros((16 - height, DEPTH), F32)], axis=0)
            local = row + 16 * b
            s = local + ROWS * g
            value = jnp.where(lane < s, value, jnp.where(lane == s, 0.5 * value, 0.0))
            if b == 4:
                value = jnp.where(local < ROWS, value, 0.0)
            hi, lo = split(value)
            th[pl.ds(BAND * p + 16 * b, 16), :] = hi
            tl[pl.ds(BAND * p + 16 * b, 16), :] = lo

    for n in range(4):
        got[n, pl.ds(NAO, DEPTH - NAO), :] = jnp.zeros((DEPTH - NAO, 128), F32)

    pl.semaphore_wait(barrier, 16 + 1 + 64 - jnp.where(src1 == c, 1, 0) - jnp.where(src2 == c, 1, 0))

    def stage1(q, carry):
        base = pl.multiple_of(q * 256, 256)
        bh = ch[pl.ds(base, 256), :]
        bl = cl[pl.ds(base, 256), :]
        acc = dot3(th[...], tl[...], bh, bl, NT)
        for e in range(2):
            sent[2 * q + e] = acc[:, 128 * e:128 * (e + 1)]
        c2 = q // 2
        wd = y * 2 + c2

        def send(k, carry):
            i = lax.rem(k // 2 + g, 8)
            e = lax.rem(k, 2)
            j = 8 * c + i
            tile = lax.rem(2 * q, 4) + e
            src = sent.at[2 * q + e, pl.ds(i * BAND, ROWS), :]
            dst = got.at[tile, pl.ds(ROWS * g, ROWS), :]

            @pl.when((j != g) | (c2 != c))
            def _():
                pltpu.make_async_remote_copy(
                    src_ref=src, dst_ref=dst, send_sem=s1.at[q, k], recv_sem=r1.at[tile, g],
                    device_id=(wd, j), device_id_type=MESH).start()

            @pl.when((j == g) & (c2 == c))
            def _():
                pltpu.make_async_copy(src, dst, l1.at[e]).start()
                pltpu.make_async_copy(src, dst, l1.at[e]).wait()
            return carry

        lax.fori_loop(0, 16, send, 0)
        return carry

    lax.fori_loop(0, 4, stage1, 0)

    for h in range(2):
        def arrive(k, carry):
            tile, gs = 2 * h + k // 16, lax.rem(k, 16)

            @pl.when((gs != g) | (src1 != c))
            def _():
                pltpu.make_async_remote_copy(
                    src_ref=sent.at[0, pl.ds(0, ROWS), :], dst_ref=got.at[tile, pl.ds(ROWS * gs, ROWS), :],
                    send_sem=s1.at[0, 0], recv_sem=r1.at[tile, gs], device_id=(w, g), device_id_type=MESH).wait_recv()
            return carry

        lax.fori_loop(0, 32, arrive, 0)

        def halves(b, carry):
            at = pl.multiple_of(b * 128, 128)
            for e in range(2):
                hi, lo = split(got[2 * h + e, pl.ds(at, 128), :])
                ah[pl.ds(at, 128), pl.ds(128 * e, 128)] = hi
                al[pl.ds(at, 128), pl.ds(128 * e, 128)] = lo
            return carry

        lax.fori_loop(0, DEPTH // 128, halves, 0)

        def rows_of(half, carry):
            at = pl.multiple_of(lax.rem(half + other, 2) * 512, 512)
            acc = dot3(ch[pl.ds(at, 512), :], cl[pl.ds(at, 512), :], ah[...], al[...], NN)
            for e in range(2):
                m[2 * h + e, pl.ds(at, 512), :] = acc[:, 128 * e:128 * (e + 1)]

            @pl.when(half == 0)
            def _():
                for e in range(2):
                    pltpu.make_async_remote_copy(
                        src_ref=m.at[2 * h + e, pl.ds(at, 512), :], dst_ref=xr.at[2 * h + e],
                        send_sem=sx.at[2 * h + e], recv_sem=rx.at[2 * h + e],
                        device_id=(y * 2 + other, g), device_id_type=MESH).start()
            return carry

        lax.fori_loop(0, 2, rows_of, 0)

    pair = 16 * y + g

    def spread(n, half, a):
        v = 4 * half + a
        wd = 4 * c + n
        for r in range(2):
            gd = 2 * v + r
            src = n_.at[n, pl.ds(v * 128 + r * KROWS, KROWS), :]
            dst = o.at[pl.ds(pair * SLOT, KROWS), :]

            @pl.when((gd != g) | (wd != w))
            def _():
                pltpu.make_async_remote_copy(
                    src_ref=src, dst_ref=dst, send_sem=s2.at[n, gd], recv_sem=r2.at[pair],
                    device_id=(wd, gd), device_id_type=MESH).start()

            @pl.when((gd == g) & (wd == w))
            def _():
                pltpu.make_async_copy(src, dst, l2).start()
                pltpu.make_async_copy(src, dst, l2).wait()

    def own(t, carry):
        n, a = t // 4, lax.rem(t, 4)
        at = pl.multiple_of((4 * c + a) * 128, 128)
        back = pl.multiple_of((4 * c + n) * 128, 128)
        n_[n, pl.ds(at, 128), :] = m[n, pl.ds(at, 128), :] + m[a, pl.ds(back, 128), :].T
        spread(n, c, a)
        return carry

    lax.fori_loop(0, 16, own, 0)

    for n in range(4):
        pltpu.make_async_remote_copy(
            src_ref=m.at[n, pl.ds(0, 512), :], dst_ref=xr.at[n], send_sem=sx.at[n], recv_sem=rx.at[n],
            device_id=(w, g), device_id_type=MESH).wait()

    def cross(t, carry):
        n, a = t // 4, lax.rem(t, 4)
        at = pl.multiple_of((4 * other + a) * 128, 128)
        n_[n, pl.ds(at, 128), :] = m[n, pl.ds(at, 128), :] + xr[a, pl.ds(pl.multiple_of(n * 128, 128), 128), :].T
        spread(n, other, a)
        return carry

    lax.fori_loop(0, 16, cross, 0)

    def left1(k, carry):
        q, kk = k // 16, lax.rem(k, 16)
        j = 8 * c + lax.rem(kk // 2 + g, 8)

        @pl.when((j != g) | (q // 2 != c))
        def _():
            pltpu.make_async_remote_copy(
                src_ref=sent.at[0, pl.ds(0, ROWS), :], dst_ref=got.at[0, pl.ds(0, ROWS), :],
                send_sem=s1.at[q, kk], recv_sem=r1.at[0, 0], device_id=(w, g), device_id_type=MESH).wait_send()
        return carry

    lax.fori_loop(0, 64, left1, 0)

    def left2(k, carry):
        n, gd = k // 16, lax.rem(k, 16)

        @pl.when((gd != g) | (4 * c + n != w))
        def _():
            pltpu.make_async_remote_copy(
                src_ref=n_.at[0, pl.ds(0, KROWS), :], dst_ref=o.at[pl.ds(0, KROWS), :],
                send_sem=s2.at[n, gd], recv_sem=r2.at[0], device_id=(w, g), device_id_type=MESH).wait_send()
        return carry

    lax.fori_loop(0, 64, left2, 0)

    def landed(q, carry):
        @pl.when((q != pair) | (src2 != c))
        def _():
            pltpu.make_async_remote_copy(
                src_ref=n_.at[0, pl.ds(0, KROWS), :], dst_ref=o.at[pl.ds(q * SLOT, KROWS), :],
                send_sem=s2.at[0, 0], recv_sem=r2.at[q], device_id=(w, g), device_id_type=MESH).wait_recv()
        return carry

    lax.fori_loop(0, PAIRS, landed, 0)

    def gather(k, carry):
        for b in range(PAIRS // 8):
            out_ref[k, pl.ds(8 * b, 8), :] = o[pl.ds(8 * b * SLOT + k, 8, stride=SLOT), :][:, :COLS]
        return carry

    lax.fori_loop(0, KROWS, gather, 0)


def on_device(integrals, coeffs):
    dma = pltpu.SemaphoreType.DMA
    slab = pl.pallas_call(
        kernel,
        out_shape=jax.ShapeDtypeStruct((KROWS, PAIRS, COLS), F32),
        in_specs=[pl.BlockSpec(memory_space=pl.ANY)] * 2,
        out_specs=pl.BlockSpec(memory_space=pltpu.VMEM),
        scratch_shapes=[
            pltpu.VMEM((OWN, ROWS, NAO), F32),
            pltpu.VMEM((816, NAO), F32),
            pltpu.VMEM((OWN * BAND, DEPTH), BF16),
            pltpu.VMEM((OWN * BAND, DEPTH), BF16),
            pltpu.VMEM((1024, DEPTH), BF16),
            pltpu.VMEM((1024, DEPTH), BF16),
            pltpu.VMEM((8, OWN * BAND, 128), F32),
            pltpu.VMEM((4, DEPTH, 128), F32),
            pltpu.VMEM((DEPTH, 256), BF16),
            pltpu.VMEM((DEPTH, 256), BF16),
            pltpu.VMEM((4, 1024, 128), F32),
            pltpu.VMEM((4, 512, 128), F32),
            pltpu.VMEM((4, 1024, 128), F32),
            pltpu.VMEM((PAIRS * SLOT, 128), F32),
            dma((OWN,)), dma,
            dma((4, 16)), dma((4, 16)), dma((2,)),
            dma((4,)), dma((4,)),
            dma((4, 16)), dma((PAIRS,)), dma,
        ],
        compiler_params=pltpu.CompilerParams(
            collective_id=0, has_side_effects=True, vmem_limit_bytes=60 * 2**20),
    )(integrals, coeffs.T)
    return jnp.transpose(slab, (0, 2, 1))


def solution(mesh):
    return jax.shard_map(
        on_device,
        mesh=mesh,
        in_specs=(P("grp", "wide", None), P()),
        out_specs=P("grp", "wide", None),
        check_vma=False,
    )
```

```python
import functools

import jax
import jax.numpy as jnp
from jax import lax
from jax.experimental import pallas as pl
from jax.experimental.pallas import tpu as pltpu
from jax.sharding import PartitionSpec as P

MESH = pl.DeviceIdType.MESH
F32 = jnp.float32
BF16 = jnp.bfloat16
NT = (((1,), (1,)), ((), ()))
NN = (((1,), (0,)), ((), ()))

ROWS = 75
BAND = 80
OWN = 8
NAO = 1200
DEPTH = 1280
COLS = 100
KROWS = 50
SLOT = 56
PAIRS = 64


def split(v):
    hi = v.astype(BF16)
    return hi, (v - hi.astype(F32)).astype(BF16)


def widen(v):
    return jnp.concatenate([v, jnp.zeros((v.shape[0], DEPTH - NAO), F32)], axis=1)


def dot3(ah, al, bh, bl, dims):
    dot = functools.partial(lax.dot_general, dimension_numbers=dims, preferred_element_type=F32)
    return dot(ah, bh) + (dot(ah, bl) + dot(al, bh))


def kernel(x_ref, ct_ref, out_ref, xbuf, cbuf, th, tl, ch, cl, sent, got, ah, al, m, xr, n_, o,
           xsem, csem, s1, r1, l1, sx, rx, s2, r2, l2, ready):
    g = lax.axis_index("grp")
    w = lax.axis_index("wide")
    y, c = w // 2, lax.rem(w, 2)
    other = 1 - c
    barrier = pltpu.get_barrier_semaphore()

    loads = [pltpu.make_async_copy(ct_ref, cbuf.at[pl.ds(0, 800), :], csem)]
    for p in range(OWN):
        loads.append(pltpu.make_async_copy(x_ref.at[:, p, :], xbuf.at[p], xsem.at[p]))
    for load in loads:
        load.start()

    src1 = g // 8
    src2 = y // 2

    def greet1(d, carry):
        gs = lax.rem(g + d, 16)

        @pl.when((d != 0) | (src1 != c))
        def _():
            pl.semaphore_signal(barrier, inc=1, device_id=(y * 2 + src1, gs), device_id_type=MESH)
        return carry

    lax.fori_loop(0, 16, greet1, 0)
    def greet2(d, carry):
        @pl.when(d != w)
        def _():
            pl.semaphore_signal(barrier, inc=1, device_id=(d, g), device_id_type=MESH)
        return carry

    lax.fori_loop(0, 8, greet2, 0)

    loads[0].wait()
    lane = lax.broadcasted_iota(jnp.int32, (16, DEPTH), 1)
    row = lax.broadcasted_iota(jnp.int32, (16, DEPTH), 0)
    for v in range(8):
        for b in range(7):
            value = widen(cbuf[pl.ds(COLS * v + 16 * b, 16), :])
            keep = lane < NAO
            if b == 6:
                keep = keep & (row < COLS - 96)
            hi, lo = split(jnp.where(keep, value, 0.0))
            ch[pl.ds(128 * v + 16 * b, 16), :] = hi
            cl[pl.ds(128 * v + 16 * b, 16), :] = lo
        ch[pl.ds(128 * v + 112, 16), :] = jnp.zeros((16, DEPTH), BF16)
        cl[pl.ds(128 * v + 112, 16), :] = jnp.zeros((16, DEPTH), BF16)

    for p in range(OWN):
        loads[1 + p].wait()
        for b in range(5):
            height = min(16, ROWS - 16 * b)
            value = widen(xbuf[p, pl.ds(16 * b, height), :])
            if height < 16:
                value = jnp.concatenate([value, jnp.zeros((16 - height, DEPTH), F32)], axis=0)
            local = row + 16 * b
            s = local + ROWS * g
            value = jnp.where(lane < s, value, jnp.where(lane == s, 0.5 * value, 0.0))
            if b == 4:
                value = jnp.where(local < ROWS, value, 0.0)
            hi, lo = split(value)
            th[pl.ds(BAND * p + 16 * b, 16), :] = hi
            tl[pl.ds(BAND * p + 16 * b, 16), :] = lo

    for n in range(4):
        got[n, pl.ds(NAO, DEPTH - NAO), :] = jnp.zeros((DEPTH - NAO, 128), F32)

    pl.semaphore_wait(barrier, 16 + 7 - jnp.where(src1 == c, 1, 0))

    def pass_on(d, carry):
        @pl.when(d != w)
        def _():
            pl.semaphore_signal(ready, inc=1, device_id=(d, g), device_id_type=MESH)
        return carry

    lax.fori_loop(0, 8, pass_on, 0)

    def stage1(q, carry):
        c2, h = lax.rem(q, 2), q // 2
        base = pl.multiple_of(c2 * 512 + h * 256, 256)
        bh = ch[pl.ds(base, 256), :]
        bl = cl[pl.ds(base, 256), :]
        acc = dot3(th[...], tl[...], bh, bl, NT)
        for e in range(2):
            sent[2 * q + e] = acc[:, 128 * e:128 * (e + 1)]
        wd = y * 2 + c2

        def send(k, carry):
            i = lax.rem(k // 2 + g, 8)
            e = lax.rem(k, 2)
            j = 8 * c + i
            tile = 2 * h + e
            src = sent.at[2 * q + e, pl.ds(i * BAND, ROWS), :]
            dst = got.at[tile, pl.ds(ROWS * g, ROWS), :]

            @pl.when((j != g) | (c2 != c))
            def _():
                pltpu.make_async_remote_copy(
                    src_ref=src, dst_ref=dst, send_sem=s1.at[q, k], recv_sem=r1.at[tile, g],
                    device_id=(wd, j), device_id_type=MESH).start()

            @pl.when((j == g) & (c2 == c))
            def _():
                pltpu.make_async_copy(src, dst, l1.at[e]).start()
                pltpu.make_async_copy(src, dst, l1.at[e]).wait()
            return carry

        lax.fori_loop(0, 16, send, 0)
        return carry

    lax.fori_loop(0, 4, stage1, 0)

    pair = 16 * y + g

    def arrive(h):
        def one(k, carry):
            tile, gs = 2 * h + k // 16, lax.rem(k, 16)

            @pl.when((gs != g) | (src1 != c))
            def _():
                pltpu.make_async_remote_copy(
                    src_ref=sent.at[0, pl.ds(0, ROWS), :], dst_ref=got.at[tile, pl.ds(ROWS * gs, ROWS), :],
                    send_sem=s1.at[0, 0], recv_sem=r1.at[tile, gs], device_id=(w, g), device_id_type=MESH).wait_recv()
            return carry

        lax.fori_loop(0, 32, one, 0)

    def multiply(h):
        def halves(b, carry):
            at = pl.multiple_of(b * 128, 128)
            for e in range(2):
                hi, lo = split(got[2 * h + e, pl.ds(at, 128), :])
                ah[pl.ds(at, 128), pl.ds(128 * e, 128)] = hi
                al[pl.ds(at, 128), pl.ds(128 * e, 128)] = lo
            return carry

        lax.fori_loop(0, DEPTH // 128, halves, 0)

        def rows_of(half, carry):
            at = pl.multiple_of(lax.rem(half + other, 2) * 512, 512)
            acc = dot3(ch[pl.ds(at, 512), :], cl[pl.ds(at, 512), :], ah[...], al[...], NN)
            for e in range(2):
                m[2 * h + e, pl.ds(at, 512), :] = acc[:, 128 * e:128 * (e + 1)]

            @pl.when(half == 0)
            def _():
                for e in range(2):
                    pltpu.make_async_remote_copy(
                        src_ref=m.at[2 * h + e, pl.ds(at, 512), :], dst_ref=xr.at[2 * h + e],
                        send_sem=sx.at[2 * h + e], recv_sem=rx.at[2 * h + e],
                        device_id=(y * 2 + other, g), device_id_type=MESH).start()
            return carry

        lax.fori_loop(0, 2, rows_of, 0)

    def crossed(h):
        for n in (2 * h, 2 * h + 1):
            pltpu.make_async_remote_copy(
                src_ref=m.at[n, pl.ds(0, 512), :], dst_ref=xr.at[n], send_sem=sx.at[n], recv_sem=rx.at[n],
                device_id=(w, g), device_id_type=MESH).wait()

    def add(across, a, n):
        half = other if across else c
        at = pl.multiple_of((4 * half + a) * 128, 128)
        if across:
            back = xr[a, pl.ds(pl.multiple_of(n * 128, 128), 128), :]
        else:
            back = m[a, pl.ds(pl.multiple_of((4 * c + n) * 128, 128), 128), :]
        n_[n, pl.ds(at, 128), :] = m[n, pl.ds(at, 128), :] + back.T

    def spread(half, a, n, r):
        v = 4 * half + a
        wd = 4 * c + n
        gd = 2 * v + r
        src = n_.at[n, pl.ds(v * 128 + r * KROWS, KROWS), :]
        dst = o.at[pl.ds(pair * SLOT, KROWS), :]

        @pl.when((gd != g) | (wd != w))
        def _():
            pltpu.make_async_remote_copy(
                src_ref=src, dst_ref=dst, send_sem=s2.at[n, gd], recv_sem=r2.at[pair],
                device_id=(wd, gd), device_id_type=MESH).start()

        @pl.when((gd == g) & (wd == w))
        def _():
            pltpu.make_async_copy(src, dst, l2).start()
            pltpu.make_async_copy(src, dst, l2).wait()

    arrive(0)
    multiply(0)
    crossed(0)

    def plain(t, carry):
        a, n = t // 4, lax.rem(t, 4)
        add(False, a, n)
        add(True, a, n)
        return carry

    pl.semaphore_wait(ready, 7)
    arrive(1)
    multiply(1)
    crossed(1)
    lax.fori_loop(0, 16, plain, 0)
    z, x = g // 4, lax.rem(g, 4)

    def out(t, carry):
        k = lax.rem(t * 11, 64)
        zd = 2 * lax.rem(k // 32 + c, 2) + lax.rem(k // 16 + z, 2)
        xd = lax.rem(k // 4 + x, 4)
        v = 2 * zd + xd // 2
        spread(zd // 2, lax.rem(v, 4), lax.rem(k + y, 4), lax.rem(xd, 2))
        return carry

    lax.fori_loop(0, 64, out, 0)

    def left1(k, carry):
        q, kk = k // 16, lax.rem(k, 16)
        j = 8 * c + lax.rem(kk // 2 + g, 8)

        @pl.when((j != g) | (lax.rem(q, 2) != c))
        def _():
            pltpu.make_async_remote_copy(
                src_ref=sent.at[0, pl.ds(0, ROWS), :], dst_ref=got.at[0, pl.ds(0, ROWS), :],
                send_sem=s1.at[q, kk], recv_sem=r1.at[0, 0], device_id=(w, g), device_id_type=MESH).wait_send()
        return carry

    lax.fori_loop(0, 64, left1, 0)

    def left2(k, carry):
        n, gd = k // 16, lax.rem(k, 16)

        @pl.when((gd != g) | (4 * c + n != w))
        def _():
            pltpu.make_async_remote_copy(
                src_ref=n_.at[0, pl.ds(0, KROWS), :], dst_ref=o.at[pl.ds(0, KROWS), :],
                send_sem=s2.at[n, gd], recv_sem=r2.at[0], device_id=(w, g), device_id_type=MESH).wait_send()
        return carry

    lax.fori_loop(0, 64, left2, 0)

    def landed(q, carry):
        @pl.when((q != pair) | (src2 != c))
        def _():
            pltpu.make_async_remote_copy(
                src_ref=n_.at[0, pl.ds(0, KROWS), :], dst_ref=o.at[pl.ds(q * SLOT, KROWS), :],
                send_sem=s2.at[0, 0], recv_sem=r2.at[q], device_id=(w, g), device_id_type=MESH).wait_recv()
        return carry

    lax.fori_loop(0, PAIRS, landed, 0)

    def gather(k, carry):
        for b in range(PAIRS // 8):
            out_ref[k, pl.ds(8 * b, 8), :] = o[pl.ds(8 * b * SLOT + k, 8, stride=SLOT), :][:, :COLS]
        return carry

    lax.fori_loop(0, KROWS, gather, 0)


def on_device(integrals, coeffs):
    dma = pltpu.SemaphoreType.DMA
    slab = pl.pallas_call(
        kernel,
        out_shape=jax.ShapeDtypeStruct((KROWS, PAIRS, COLS), F32),
        in_specs=[pl.BlockSpec(memory_space=pl.ANY)] * 2,
        out_specs=pl.BlockSpec(memory_space=pltpu.VMEM),
        scratch_shapes=[
            pltpu.VMEM((OWN, ROWS, NAO), F32),
            pltpu.VMEM((816, NAO), F32),
            pltpu.VMEM((OWN * BAND, DEPTH), BF16),
            pltpu.VMEM((OWN * BAND, DEPTH), BF16),
            pltpu.VMEM((1024, DEPTH), BF16),
            pltpu.VMEM((1024, DEPTH), BF16),
            pltpu.VMEM((8, OWN * BAND, 128), F32),
            pltpu.VMEM((4, DEPTH, 128), F32),
            pltpu.VMEM((DEPTH, 256), BF16),
            pltpu.VMEM((DEPTH, 256), BF16),
            pltpu.VMEM((4, 1024, 128), F32),
            pltpu.VMEM((4, 512, 128), F32),
            pltpu.VMEM((4, 1024, 128), F32),
            pltpu.VMEM((PAIRS * SLOT, 128), F32),
            dma((OWN,)), dma,
            dma((4, 16)), dma((4, 16)), dma((2,)),
            dma((4,)), dma((4,)),
            dma((4, 16)), dma((PAIRS,)), dma, pltpu.SemaphoreType.REGULAR,
        ],
        compiler_params=pltpu.CompilerParams(
            collective_id=0, has_side_effects=True, vmem_limit_bytes=60 * 2**20),
    )(integrals, coeffs.T)
    return jnp.transpose(slab, (0, 2, 1))


def solution(mesh):
    return jax.shard_map(
        on_device,
        mesh=mesh,
        in_specs=(P("grp", "wide", None), P()),
        out_specs=P("grp", "wide", None),
        check_vma=False,
    )
```

```python
import functools

import jax
import jax.numpy as jnp
from jax import lax
from jax.experimental import pallas as pl
from jax.experimental.pallas import tpu as pltpu
from jax.sharding import PartitionSpec as P

MESH = pl.DeviceIdType.MESH
F32 = jnp.float32
BF16 = jnp.bfloat16
NT = (((1,), (1,)), ((), ()))
NN = (((1,), (0,)), ((), ()))

ROWS = 75
BAND = 80
OWN = 8
NAO = 1200
DEPTH = 1280
COLS = 100
KROWS = 50
PAIRS = 64


def split(v):
    hi = v.astype(BF16)
    return hi, (v - hi.astype(F32)).astype(BF16)


def widen(v):
    return jnp.concatenate([v, jnp.zeros((v.shape[0], DEPTH - NAO), F32)], axis=1)


def dot3(ah, al, bh, bl, dims):
    dot = functools.partial(lax.dot_general, dimension_numbers=dims, preferred_element_type=F32)
    return dot(ah, bh) + (dot(ah, bl) + dot(al, bh))


def kernel(x_ref, ct_ref, o, xbuf, cbuf, th, tl, fh, fl, ch, cl, sent, sentl, got, gotl, ah, al, m, xr, n_,
           xsem, csem, s1, r1, l1, sx, rx, s2, r2, l2, ready):
    g = lax.axis_index("grp")
    w = lax.axis_index("wide")
    y, c = w // 2, lax.rem(w, 2)
    other = 1 - c
    barrier = pltpu.get_barrier_semaphore()

    loads = [pltpu.make_async_copy(ct_ref, cbuf.at[pl.ds(0, 800), :], csem)]
    for p in range(OWN):
        loads.append(pltpu.make_async_copy(x_ref.at[:, p, :], xbuf.at[p], xsem.at[p]))
    for load in loads:
        load.start()

    src1 = g // 8
    src2 = y // 2

    def greet1(d, carry):
        gs = lax.rem(g + d, 16)

        @pl.when((d != 0) | (src1 != c))
        def _():
            pl.semaphore_signal(barrier, inc=1, device_id=(y * 2 + src1, gs), device_id_type=MESH)
        return carry

    lax.fori_loop(0, 16, greet1, 0)
    def greet2(d, carry):
        @pl.when(d != w)
        def _():
            pl.semaphore_signal(barrier, inc=1, device_id=(d, g), device_id_type=MESH)
        return carry

    lax.fori_loop(0, 8, greet2, 0)

    loads[0].wait()
    lane = lax.broadcasted_iota(jnp.int32, (16, DEPTH), 1)
    row = lax.broadcasted_iota(jnp.int32, (16, DEPTH), 0)

    def flat(b, carry):
        at = pl.multiple_of(16 * b, 16)
        hi, lo = split(widen(cbuf[pl.ds(at, 16), :]))
        fh[pl.ds(at, 16), :] = hi
        fl[pl.ds(at, 16), :] = lo
        return carry

    lax.fori_loop(0, 50, flat, 0)
    fh[pl.ds(800, 112), :] = jnp.zeros((112, DEPTH), BF16)
    fl[pl.ds(800, 112), :] = jnp.zeros((112, DEPTH), BF16)

    for p in range(OWN):
        loads[1 + p].wait()
        for b in range(5):
            height = min(16, ROWS - 16 * b)
            value = widen(xbuf[p, pl.ds(16 * b, height), :])
            if height < 16:
                value = jnp.concatenate([value, jnp.zeros((16 - height, DEPTH), F32)], axis=0)
            local = row + 16 * b
            s = local + ROWS * g
            value = jnp.where(lane < s, value, jnp.where(lane == s, 0.5 * value, 0.0))
            if b == 4:
                value = jnp.where(local < ROWS, value, 0.0)
            hi, lo = split(value)
            th[pl.ds(BAND * p + 16 * b, 16), :] = hi
            tl[pl.ds(BAND * p + 16 * b, 16), :] = lo

    for n in range(4):
        got[n, pl.ds(NAO, DEPTH - NAO), :] = jnp.zeros((DEPTH - NAO, 128), F32)

    narrow = lax.broadcasted_iota(jnp.int32, (8, 128), 1) < 16

    def stage1(q, carry):
        c2, h = lax.rem(q, 2), q // 2
        base = pl.multiple_of(c2 * 400 + h * 256, 16)
        acc = dot3(th[...], tl[...], fh[pl.ds(base, 256), :], fl[pl.ds(base, 256), :], NT)
        sent[2 * q] = acc[:, :128]

        @pl.when(h == 0)
        def _():
            sent[2 * q + 1] = acc[:, 128:]

        @pl.when(h == 1)
        def _():
            for i in range(OWN):
                parts = [jnp.where(narrow, acc[BAND * i + 8 * b:BAND * i + 8 * b + 8, 128:], 0.0) for b in range(10)]
                first = parts[0]
                for b in range(1, 8):
                    first = first + pltpu.roll(parts[b], 16 * b, 1)
                sentl[c2, pl.ds(16 * i, 8), :] = first
                sentl[c2, pl.ds(16 * i + 8, 8), :] = parts[8] + pltpu.roll(parts[9], 16, 1)

        @pl.when(q == 0)
        def _():
            pl.semaphore_wait(barrier, 16 + 7 - jnp.where(src1 == c, 1, 0))

        wd = y * 2 + c2

        def put(src, dst, j, k, tile):
            @pl.when((j != g) | (c2 != c))
            def _():
                pltpu.make_async_remote_copy(
                    src_ref=src, dst_ref=dst, send_sem=s1.at[q, k], recv_sem=r1.at[tile, g],
                    device_id=(wd, j), device_id_type=MESH).start()

            @pl.when((j == g) & (c2 == c))
            def _():
                pltpu.make_async_copy(src, dst, l1).start()
                pltpu.make_async_copy(src, dst, l1).wait()

        def send(k, carry):
            i = lax.rem(k // 2 + g, 8)
            e = lax.rem(k, 2)
            j = 8 * c + i
            tile = 2 * h + e

            @pl.when(tile < 3)
            def _():
                put(sent.at[2 * q + e, pl.ds(i * BAND, ROWS), :], got.at[tile, pl.ds(ROWS * g, ROWS), :], j, k, tile)

            @pl.when(tile == 3)
            def _():
                put(sentl.at[c2, pl.ds(16 * i, 16), :], gotl.at[pl.ds(16 * g, 16), :], j, k, tile)
            return carry

        lax.fori_loop(0, 16, send, 0)
        return carry

    lax.fori_loop(0, 4, stage1, 0)

    def pass_on(d, carry):
        @pl.when(d != w)
        def _():
            pl.semaphore_signal(ready, inc=1, device_id=(d, g), device_id_type=MESH)
        return carry

    lax.fori_loop(0, 8, pass_on, 0)

    for v in range(8):
        for b in range(7):
            value = widen(cbuf[pl.ds(COLS * v + 16 * b, 16), :])
            if b == 6:
                value = jnp.where(row < COLS - 96, value, 0.0)
            hi, lo = split(value)
            ch[pl.ds(128 * v + 16 * b, 16), :] = hi
            cl[pl.ds(128 * v + 16 * b, 16), :] = lo
        ch[pl.ds(128 * v + 112, 16), :] = jnp.zeros((16, DEPTH), BF16)
        cl[pl.ds(128 * v + 112, 16), :] = jnp.zeros((16, DEPTH), BF16)

    pair = 16 * y + g

    def arrive(h):
        for tile in (2 * h, 2 * h + 1):
            def one(gs, carry):
                @pl.when((gs != g) | (src1 != c))
                def _():
                    if tile < 3:
                        src, dst = sent.at[0, pl.ds(0, ROWS), :], got.at[tile, pl.ds(ROWS * gs, ROWS), :]
                    else:
                        src, dst = sentl.at[0, pl.ds(0, 16), :], gotl.at[pl.ds(16 * gs, 16), :]
                    pltpu.make_async_remote_copy(
                        src_ref=src, dst_ref=dst, send_sem=s1.at[0, 0], recv_sem=r1.at[tile, gs],
                        device_id=(w, g), device_id_type=MESH).wait_recv()
                return carry

            lax.fori_loop(0, 16, one, 0)

    def multiply(h):
        if h == 1:
            for gs in range(16):
                for b in range(10):
                    part = gotl[pl.ds(16 * gs + 8 * (b // 8), 8), :]
                    if b % 8:
                        part = pltpu.roll(part, 128 - 16 * (b % 8), 1)
                    got[3, pl.ds(ROWS * gs + 8 * b, 8), :] = part

        def halves(b, carry):
            at = pl.multiple_of(b * 128, 128)
            here = lax.broadcasted_iota(jnp.int32, (128, 128), 1)
            for e in range(2):
                n = 2 * h + e
                value = got[n, pl.ds(at, 128), :]
                if n:
                    before = got[n - 1, pl.ds(at, 128), :]
                    value = jnp.where(here < 28 * n, pltpu.roll(before, 28 * n, 1), pltpu.roll(value, 28 * n, 1))
                hi, lo = split(value)
                ah[pl.ds(at, 128), pl.ds(128 * e, 128)] = hi
                al[pl.ds(at, 128), pl.ds(128 * e, 128)] = lo
            return carry

        lax.fori_loop(0, DEPTH // 128, halves, 0)

        def rows_of(half, carry):
            at = pl.multiple_of(lax.rem(half + other, 2) * 512, 512)
            acc = dot3(ch[pl.ds(at, 512), :], cl[pl.ds(at, 512), :], ah[...], al[...], NN)
            for e in range(2):
                m[2 * h + e, pl.ds(at, 512), :] = acc[:, 128 * e:128 * (e + 1)]

            @pl.when(half == 0)
            def _():
                for e in range(2):
                    pltpu.make_async_remote_copy(
                        src_ref=m.at[2 * h + e, pl.ds(at, 512), :], dst_ref=xr.at[2 * h + e],
                        send_sem=sx.at[2 * h + e], recv_sem=rx.at[2 * h + e],
                        device_id=(y * 2 + other, g), device_id_type=MESH).start()
            return carry

        lax.fori_loop(0, 2, rows_of, 0)

    def crossed(h):
        for n in (2 * h, 2 * h + 1):
            pltpu.make_async_remote_copy(
                src_ref=m.at[n, pl.ds(0, 512), :], dst_ref=xr.at[n], send_sem=sx.at[n], recv_sem=rx.at[n],
                device_id=(w, g), device_id_type=MESH).wait()

    def add(across, a, n):
        half = other if across else c
        at = pl.multiple_of((4 * half + a) * 128, 128)
        if across:
            back = xr[a, pl.ds(pl.multiple_of(n * 128, 128), 128), :]
        else:
            back = m[a, pl.ds(pl.multiple_of((4 * c + n) * 128, 128), 128), :]
        n_[n, pl.ds(at, 128), :] = m[n, pl.ds(at, 128), :] + back.T

    def spread(half, a, n, r):
        v = 4 * half + a
        wd = 4 * c + n
        gd = 2 * v + r
        src = n_.at[n, pl.ds(v * 128 + r * KROWS, KROWS), :]
        dst = o.at[:, pair, :]

        @pl.when((gd != g) | (wd != w))
        def _():
            pltpu.make_async_remote_copy(
                src_ref=src, dst_ref=dst, send_sem=s2.at[n, gd], recv_sem=r2.at[pair],
                device_id=(wd, gd), device_id_type=MESH).start()

        @pl.when((gd == g) & (wd == w))
        def _():
            pltpu.make_async_copy(src, dst, l2).start()
            pltpu.make_async_copy(src, dst, l2).wait()

    arrive(0)
    multiply(0)
    crossed(0)

    pl.semaphore_wait(ready, 7)
    arrive(1)
    multiply(1)
    crossed(1)
    z, x = g // 4, lax.rem(g, 4)

    def out(t, carry):
        k = lax.rem(t * 11, 64)
        zd = 2 * lax.rem(k // 32 + c, 2) + lax.rem(k // 16 + z, 2)
        xd = lax.rem(k // 4 + x, 4)
        n = lax.rem(k + y, 4)
        half, r = zd // 2, lax.rem(xd, 2)
        a = 2 * lax.rem(zd, 2) + xd // 2
        twin = 16 * (k // 16) + 4 * lax.rem(xd + 1 - 2 * r + 4 - x, 4) + lax.rem(k, 4)
        first = t < lax.rem(twin * 35, 64)

        @pl.when(first & (half == c))
        def _():
            add(False, a, n)

        @pl.when(first & (half != c))
        def _():
            add(True, a, n)

        spread(half, a, n, r)
        return carry

    lax.fori_loop(0, 64, out, 0)

    def left1(k, carry):
        q, kk = k // 16, lax.rem(k, 16)
        j = 8 * c + lax.rem(kk // 2 + g, 8)
        last = (q >= 2) & (lax.rem(kk, 2) == 1)
        moved = (j != g) | (lax.rem(q, 2) != c)

        def gone(src):
            pltpu.make_async_remote_copy(
                src_ref=src, dst_ref=src, send_sem=s1.at[q, kk], recv_sem=r1.at[0, 0],
                device_id=(w, g), device_id_type=MESH).wait_send()

        @pl.when(moved & jnp.logical_not(last))
        def _():
            gone(sent.at[0, pl.ds(0, ROWS), :])

        @pl.when(moved & last)
        def _():
            gone(sentl.at[0, pl.ds(0, 16), :])
        return carry

    lax.fori_loop(0, 64, left1, 0)

    def left2(k, carry):
        n, gd = k // 16, lax.rem(k, 16)

        @pl.when((gd != g) | (4 * c + n != w))
        def _():
            pltpu.make_async_remote_copy(
                src_ref=n_.at[0, pl.ds(0, KROWS), :], dst_ref=o.at[:, 0, :],
                send_sem=s2.at[n, gd], recv_sem=r2.at[0], device_id=(w, g), device_id_type=MESH).wait_send()
        return carry

    lax.fori_loop(0, 64, left2, 0)

    def landed(q, carry):
        @pl.when((q != pair) | (src2 != c))
        def _():
            pltpu.make_async_remote_copy(
                src_ref=n_.at[0, pl.ds(0, KROWS), :], dst_ref=o.at[:, q, :],
                send_sem=s2.at[0, 0], recv_sem=r2.at[q], device_id=(w, g), device_id_type=MESH).wait_recv()
        return carry

    lax.fori_loop(0, PAIRS, landed, 0)


def arrange(o_ref, out_ref):
    out_ref[...] = o_ref[:, :, :COLS]


def on_device(integrals, coeffs):
    dma = pltpu.SemaphoreType.DMA
    blocks = pl.pallas_call(
        kernel,
        out_shape=jax.ShapeDtypeStruct((KROWS, PAIRS, 128), F32),
        in_specs=[pl.BlockSpec(memory_space=pl.ANY)] * 2,
        out_specs=pl.BlockSpec(memory_space=pl.ANY),
        scratch_shapes=[
            pltpu.VMEM((OWN, ROWS, NAO), F32),
            pltpu.VMEM((816, NAO), F32),
            pltpu.VMEM((OWN * BAND, DEPTH), BF16),
            pltpu.VMEM((OWN * BAND, DEPTH), BF16),
            pltpu.VMEM((912, DEPTH), BF16),
            pltpu.VMEM((912, DEPTH), BF16),
            pltpu.VMEM((1024, DEPTH), BF16),
            pltpu.VMEM((1024, DEPTH), BF16),
            pltpu.VMEM((8, OWN * BAND, 128), F32),
            pltpu.VMEM((2, OWN * 16, 128), F32),
            pltpu.VMEM((4, DEPTH, 128), F32),
            pltpu.VMEM((256, 128), F32),
            pltpu.VMEM((DEPTH, 256), BF16),
            pltpu.VMEM((DEPTH, 256), BF16),
            pltpu.VMEM((4, 1024, 128), F32),
            pltpu.VMEM((4, 512, 128), F32),
            pltpu.VMEM((4, 1024, 128), F32),
            dma((OWN,)), dma,
            dma((4, 16)), dma((4, 16)), dma,
            dma((4,)), dma((4,)),
            dma((4, 16)), dma((PAIRS,)), dma, pltpu.SemaphoreType.REGULAR,
        ],
        compiler_params=pltpu.CompilerParams(
            collective_id=0, has_side_effects=True, vmem_limit_bytes=60 * 2**20),
    )(integrals, coeffs.T)
    slab = blocks[:, :, :COLS]
    return jnp.transpose(slab, (0, 2, 1))


def solution(mesh):
    return jax.shard_map(
        on_device,
        mesh=mesh,
        in_specs=(P("grp", "wide", None), P()),
        out_specs=P("grp", "wide", None),
        check_vma=False,
    )
```

```python
import functools

import jax
import jax.numpy as jnp
from jax import lax
from jax.experimental import pallas as pl
from jax.experimental.pallas import tpu as pltpu
from jax.sharding import PartitionSpec as P

MESH = pl.DeviceIdType.MESH
F32 = jnp.float32
BF16 = jnp.bfloat16
NT = (((1,), (1,)), ((), ()))
NN = (((1,), (0,)), ((), ()))

ROWS = 75
BAND = 80
OWN = 8
NAO = 1200
DEPTH = 1280
COLS = 100
KROWS = 50
PAIRS = 64
SENT = 42
SLOT = 48


def split(v):
    hi = v.astype(BF16)
    return hi, (v - hi.astype(F32)).astype(BF16)


def widen(v):
    return jnp.concatenate([v, jnp.zeros((v.shape[0], DEPTH - NAO), F32)], axis=1)


def dot3(ah, al, bh, bl, dims):
    dot = functools.partial(lax.dot_general, dimension_numbers=dims, preferred_element_type=F32)
    return dot(ah, bh) + (dot(ah, bl) + dot(al, bh))


def kernel(x_ref, ct_ref, o, xbuf, cbuf, th, tl, fh, fl, ch, cl, sent, sentl, got, gotl, ah, al, m, xr, whole, n_,
           xsem, csem, s1, r1, l1, sx, rx, s2, r2, l2, ready):
    g = lax.axis_index("grp")
    w = lax.axis_index("wide")
    y, c = w // 2, lax.rem(w, 2)
    other = 1 - c
    barrier = pltpu.get_barrier_semaphore()

    loads = [pltpu.make_async_copy(ct_ref, cbuf.at[pl.ds(0, 800), :], csem)]
    for p in range(OWN):
        loads.append(pltpu.make_async_copy(x_ref.at[:, p, :], xbuf.at[p], xsem.at[p]))
    for load in loads:
        load.start()

    src1 = g // 8
    src2 = y // 2

    def greet1(d, carry):
        gs = lax.rem(g + d, 16)

        @pl.when((d != 0) | (src1 != c))
        def _():
            pl.semaphore_signal(barrier, inc=1, device_id=(y * 2 + src1, gs), device_id_type=MESH)
        return carry

    lax.fori_loop(0, 16, greet1, 0)
    def greet2(d, carry):
        @pl.when(d != w)
        def _():
            pl.semaphore_signal(barrier, inc=1, device_id=(d, g), device_id_type=MESH)
        return carry

    lax.fori_loop(0, 8, greet2, 0)

    loads[0].wait()
    lane = lax.broadcasted_iota(jnp.int32, (16, DEPTH), 1)
    row = lax.broadcasted_iota(jnp.int32, (16, DEPTH), 0)

    def flat(b, carry):
        at = pl.multiple_of(16 * b, 16)
        hi, lo = split(widen(cbuf[pl.ds(at, 16), :]))
        fh[pl.ds(at, 16), :] = hi
        fl[pl.ds(at, 16), :] = lo
        return carry

    lax.fori_loop(0, 50, flat, 0)
    fh[pl.ds(800, 112), :] = jnp.zeros((112, DEPTH), BF16)
    fl[pl.ds(800, 112), :] = jnp.zeros((112, DEPTH), BF16)

    for p in range(OWN):
        loads[1 + p].wait()
        for b in range(5):
            height = min(16, ROWS - 16 * b)
            value = widen(xbuf[p, pl.ds(16 * b, height), :])
            if height < 16:
                value = jnp.concatenate([value, jnp.zeros((16 - height, DEPTH), F32)], axis=0)
            local = row + 16 * b
            s = local + ROWS * g
            value = jnp.where(lane < s, value, jnp.where(lane == s, 0.5 * value, 0.0))
            if b == 4:
                value = jnp.where(local < ROWS, value, 0.0)
            hi, lo = split(value)
            th[pl.ds(BAND * p + 16 * b, 16), :] = hi
            tl[pl.ds(BAND * p + 16 * b, 16), :] = lo

    for n in range(4):
        got[n, pl.ds(NAO, DEPTH - NAO), :] = jnp.zeros((DEPTH - NAO, 128), F32)

    narrow = lax.broadcasted_iota(jnp.int32, (8, 128), 1) < 16

    def stage1(q, carry):
        c2, h = lax.rem(q, 2), q // 2
        base = pl.multiple_of(c2 * 400 + h * 256, 16)
        acc = dot3(th[...], tl[...], fh[pl.ds(base, 256), :], fl[pl.ds(base, 256), :], NT)
        sent[2 * q] = acc[:, :128]

        @pl.when(h == 0)
        def _():
            sent[2 * q + 1] = acc[:, 128:]

        @pl.when(h == 1)
        def _():
            for i in range(OWN):
                parts = [jnp.where(narrow, acc[BAND * i + 8 * b:BAND * i + 8 * b + 8, 128:], 0.0) for b in range(10)]
                first = parts[0]
                for b in range(1, 8):
                    first = first + pltpu.roll(parts[b], 16 * b, 1)
                sentl[c2, pl.ds(16 * i, 8), :] = first
                sentl[c2, pl.ds(16 * i + 8, 8), :] = parts[8] + pltpu.roll(parts[9], 16, 1)

        @pl.when(q == 0)
        def _():
            pl.semaphore_wait(barrier, 16 + 7 - jnp.where(src1 == c, 1, 0))

        wd = y * 2 + c2

        def put(src, dst, j, k, tile):
            @pl.when((j != g) | (c2 != c))
            def _():
                pltpu.make_async_remote_copy(
                    src_ref=src, dst_ref=dst, send_sem=s1.at[q, k], recv_sem=r1.at[tile, g],
                    device_id=(wd, j), device_id_type=MESH).start()

            @pl.when((j == g) & (c2 == c))
            def _():
                pltpu.make_async_copy(src, dst, l1).start()
                pltpu.make_async_copy(src, dst, l1).wait()

        def send(k, carry):
            i = lax.rem(k // 2 + g, 8)
            e = lax.rem(k, 2)
            j = 8 * c + i
            tile = 2 * h + e

            @pl.when(tile < 3)
            def _():
                put(sent.at[2 * q + e, pl.ds(i * BAND, ROWS), :], got.at[tile, pl.ds(ROWS * g, ROWS), :], j, k, tile)

            @pl.when(tile == 3)
            def _():
                put(sentl.at[c2, pl.ds(16 * i, 16), :], gotl.at[pl.ds(16 * g, 16), :], j, k, tile)
            return carry

        lax.fori_loop(0, 16, send, 0)
        return carry

    lax.fori_loop(0, 4, stage1, 0)

    def pass_on(d, carry):
        @pl.when(d != w)
        def _():
            pl.semaphore_signal(ready, inc=1, device_id=(d, g), device_id_type=MESH)
        return carry

    lax.fori_loop(0, 8, pass_on, 0)

    for v in range(8):
        for b in range(7):
            value = widen(cbuf[pl.ds(COLS * v + 16 * b, 16), :])
            if b == 6:
                value = jnp.where(row < COLS - 96, value, 0.0)
            hi, lo = split(value)
            ch[pl.ds(128 * v + 16 * b, 16), :] = hi
            cl[pl.ds(128 * v + 16 * b, 16), :] = lo
        ch[pl.ds(128 * v + 112, 16), :] = jnp.zeros((16, DEPTH), BF16)
        cl[pl.ds(128 * v + 112, 16), :] = jnp.zeros((16, DEPTH), BF16)

    pair = 16 * y + g

    def arrive(h):
        for tile in (2 * h, 2 * h + 1):
            def one(gs, carry):
                @pl.when((gs != g) | (src1 != c))
                def _():
                    if tile < 3:
                        src, dst = sent.at[0, pl.ds(0, ROWS), :], got.at[tile, pl.ds(ROWS * gs, ROWS), :]
                    else:
                        src, dst = sentl.at[0, pl.ds(0, 16), :], gotl.at[pl.ds(16 * gs, 16), :]
                    pltpu.make_async_remote_copy(
                        src_ref=src, dst_ref=dst, send_sem=s1.at[0, 0], recv_sem=r1.at[tile, gs],
                        device_id=(w, g), device_id_type=MESH).wait_recv()
                return carry

            lax.fori_loop(0, 16, one, 0)

    def multiply(h):
        if h == 1:
            for gs in range(16):
                for b in range(10):
                    part = gotl[pl.ds(16 * gs + 8 * (b // 8), 8), :]
                    if b % 8:
                        part = pltpu.roll(part, 128 - 16 * (b % 8), 1)
                    got[3, pl.ds(ROWS * gs + 8 * b, 8), :] = part

        def halves(b, carry):
            at = pl.multiple_of(b * 128, 128)
            here = lax.broadcasted_iota(jnp.int32, (128, 128), 1)
            for e in range(2):
                n = 2 * h + e
                value = got[n, pl.ds(at, 128), :]
                if n:
                    before = got[n - 1, pl.ds(at, 128), :]
                    value = jnp.where(here < 28 * n, pltpu.roll(before, 28 * n, 1), pltpu.roll(value, 28 * n, 1))
                hi, lo = split(value)
                ah[pl.ds(at, 128), pl.ds(128 * e, 128)] = hi
                al[pl.ds(at, 128), pl.ds(128 * e, 128)] = lo
            return carry

        lax.fori_loop(0, DEPTH // 128, halves, 0)

        def rows_of(half, carry):
            at = pl.multiple_of(lax.rem(half + other, 2) * 512, 512)
            acc = dot3(ch[pl.ds(at, 512), :], cl[pl.ds(at, 512), :], ah[...], al[...], NN)
            for e in range(2):
                m[2 * h + e, pl.ds(at, 512), :] = acc[:, 128 * e:128 * (e + 1)]

            @pl.when(half == 0)
            def _():
                for e in range(2):
                    pltpu.make_async_remote_copy(
                        src_ref=m.at[2 * h + e, pl.ds(at, 512), :], dst_ref=xr.at[2 * h + e],
                        send_sem=sx.at[2 * h + e], recv_sem=rx.at[2 * h + e],
                        device_id=(y * 2 + other, g), device_id_type=MESH).start()
            return carry

        lax.fori_loop(0, 2, rows_of, 0)

    def crossed(h):
        for n in (2 * h, 2 * h + 1):
            pltpu.make_async_remote_copy(
                src_ref=m.at[n, pl.ds(0, 512), :], dst_ref=xr.at[n], send_sem=sx.at[n], recv_sem=rx.at[n],
                device_id=(w, g), device_id_type=MESH).wait()

    main = lax.broadcasted_iota(jnp.int32, (8, 128), 1) < COLS

    def add(across, a, n):
        half = other if across else c
        at = pl.multiple_of((4 * half + a) * 128, 128)
        if across:
            back = xr[a, pl.ds(pl.multiple_of(n * 128, 128), 128), :]
        else:
            back = m[a, pl.ds(pl.multiple_of((4 * c + n) * 128, 128), 128), :]
        whole[...] = m[n, pl.ds(at, 128), :] + back.T
        for r in range(2):
            slot = 2 * (4 * half + a) + r
            rest = whole[pl.ds(KROWS * r + SENT, 8), :]
            for j in range(4):
                n_[n, slot, pl.ds(8 * j, 8), :] = jnp.where(
                    main, whole[pl.ds(KROWS * r + 8 * j, 8), :], pltpu.roll(rest, COLS - 25 * j, 1))
            n_[n, slot, pl.ds(32, SENT - 32), :] = whole[pl.ds(KROWS * r + 32, SENT - 32), :]

    def spread(half, a, n, r):
        v = 4 * half + a
        wd = 4 * c + n
        gd = 2 * v + r
        src = n_.at[n, gd, pl.ds(0, SENT), :]
        dst = o.at[pl.ds(pair * SLOT, SENT), :]

        @pl.when((gd != g) | (wd != w))
        def _():
            pltpu.make_async_remote_copy(
                src_ref=src, dst_ref=dst, send_sem=s2.at[n, gd], recv_sem=r2.at[pair],
                device_id=(wd, gd), device_id_type=MESH).start()

        @pl.when((gd == g) & (wd == w))
        def _():
            pltpu.make_async_copy(src, dst, l2).start()
            pltpu.make_async_copy(src, dst, l2).wait()

    arrive(0)
    multiply(0)
    crossed(0)

    pl.semaphore_wait(ready, 7)
    arrive(1)
    multiply(1)
    crossed(1)
    z, x = g // 4, lax.rem(g, 4)

    def out(t, carry):
        k = lax.rem(t * 11, 64)
        zd = 2 * lax.rem(k // 32 + c, 2) + lax.rem(k // 16 + z, 2)
        xd = lax.rem(k // 4 + x, 4)
        n = lax.rem(k + y, 4)
        half, r = zd // 2, lax.rem(xd, 2)
        a = 2 * lax.rem(zd, 2) + xd // 2
        twin = 16 * (k // 16) + 4 * lax.rem(xd + 1 - 2 * r + 4 - x, 4) + lax.rem(k, 4)
        first = t < lax.rem(twin * 35, 64)

        @pl.when(first & (half == c))
        def _():
            add(False, a, n)

        @pl.when(first & (half != c))
        def _():
            add(True, a, n)

        spread(half, a, n, r)
        return carry

    lax.fori_loop(0, 64, out, 0)

    def left1(k, carry):
        q, kk = k // 16, lax.rem(k, 16)
        j = 8 * c + lax.rem(kk // 2 + g, 8)
        last = (q >= 2) & (lax.rem(kk, 2) == 1)
        moved = (j != g) | (lax.rem(q, 2) != c)

        def gone(src):
            pltpu.make_async_remote_copy(
                src_ref=src, dst_ref=src, send_sem=s1.at[q, kk], recv_sem=r1.at[0, 0],
                device_id=(w, g), device_id_type=MESH).wait_send()

        @pl.when(moved & jnp.logical_not(last))
        def _():
            gone(sent.at[0, pl.ds(0, ROWS), :])

        @pl.when(moved & last)
        def _():
            gone(sentl.at[0, pl.ds(0, 16), :])
        return carry

    lax.fori_loop(0, 64, left1, 0)

    def left2(k, carry):
        n, gd = k // 16, lax.rem(k, 16)

        @pl.when((gd != g) | (4 * c + n != w))
        def _():
            pltpu.make_async_remote_copy(
                src_ref=n_.at[0, 0, pl.ds(0, SENT), :], dst_ref=o.at[pl.ds(0, SENT), :],
                send_sem=s2.at[n, gd], recv_sem=r2.at[0], device_id=(w, g), device_id_type=MESH).wait_send()
        return carry

    lax.fori_loop(0, 64, left2, 0)

    def landed(q, carry):
        @pl.when((q != pair) | (src2 != c))
        def _():
            pltpu.make_async_remote_copy(
                src_ref=n_.at[0, 0, pl.ds(0, SENT), :], dst_ref=o.at[pl.ds(q * SLOT, SENT), :],
                send_sem=s2.at[0, 0], recv_sem=r2.at[q], device_id=(w, g), device_id_type=MESH).wait_recv()
        return carry

    lax.fori_loop(0, PAIRS, landed, 0)


def arrange(o_ref, out_ref):
    def plain(k, carry):
        for b in range(PAIRS // 8):
            out_ref[k, pl.ds(8 * b, 8), :] = o_ref[pl.ds(8 * b * SLOT + k, 8, stride=SLOT), :][:, :COLS]
        return carry

    lax.fori_loop(0, SENT, plain, 0, unroll=6)
    lane = lax.broadcasted_iota(jnp.int32, (8, 128), 1)

    def parts(q, carry):
        for b in range(PAIRS // 8):
            value = jnp.zeros((8, 128), F32)
            for j in range(4):
                part = o_ref[pl.ds(8 * b * SLOT + 8 * j + q, 8, stride=SLOT), :]
                part = pltpu.roll(part, 28 + 25 * j, 1)
                value = part if j == 0 else jnp.where(lane >= 25 * j, part, value)
            out_ref[SENT + q, pl.ds(8 * b, 8), :] = value[:, :COLS]
        return carry

    lax.fori_loop(0, 8, parts, 0, unroll=2)


def on_device(integrals, coeffs):
    dma = pltpu.SemaphoreType.DMA
    blocks = pl.pallas_call(
        kernel,
        out_shape=jax.ShapeDtypeStruct((PAIRS * SLOT, 128), F32),
        in_specs=[pl.BlockSpec(memory_space=pl.ANY)] * 2,
        out_specs=pl.BlockSpec(memory_space=pl.ANY),
        scratch_shapes=[
            pltpu.VMEM((OWN, ROWS, NAO), F32),
            pltpu.VMEM((816, NAO), F32),
            pltpu.VMEM((OWN * BAND, DEPTH), BF16),
            pltpu.VMEM((OWN * BAND, DEPTH), BF16),
            pltpu.VMEM((912, DEPTH), BF16),
            pltpu.VMEM((912, DEPTH), BF16),
            pltpu.VMEM((1024, DEPTH), BF16),
            pltpu.VMEM((1024, DEPTH), BF16),
            pltpu.VMEM((8, OWN * BAND, 128), F32),
            pltpu.VMEM((2, OWN * 16, 128), F32),
            pltpu.VMEM((4, DEPTH, 128), F32),
            pltpu.VMEM((256, 128), F32),
            pltpu.VMEM((DEPTH, 256), BF16),
            pltpu.VMEM((DEPTH, 256), BF16),
            pltpu.VMEM((4, 1024, 128), F32),
            pltpu.VMEM((4, 512, 128), F32),
            pltpu.VMEM((128, 128), F32),
            pltpu.VMEM((4, 16, SLOT, 128), F32),
            dma((OWN,)), dma,
            dma((4, 16)), dma((4, 16)), dma,
            dma((4,)), dma((4,)),
            dma((4, 16)), dma((PAIRS,)), dma, pltpu.SemaphoreType.REGULAR,
        ],
        compiler_params=pltpu.CompilerParams(
            collective_id=0, has_side_effects=True, vmem_limit_bytes=60 * 2**20),
    )(integrals, coeffs.T)
    slab = pl.pallas_call(
        arrange,
        out_shape=jax.ShapeDtypeStruct((KROWS, PAIRS, COLS), F32),
        in_specs=[pl.BlockSpec(memory_space=pltpu.VMEM)],
        out_specs=pl.BlockSpec(memory_space=pltpu.VMEM),
    )(blocks)
    return jnp.transpose(slab, (0, 2, 1))


def solution(mesh):
    return jax.shard_map(
        on_device,
        mesh=mesh,
        in_specs=(P("grp", "wide", None), P()),
        out_specs=P("grp", "wide", None),
        check_vma=False,
    )
```

```python
import functools

import jax
import jax.numpy as jnp
from jax import lax
from jax.experimental import pallas as pl
from jax.experimental.pallas import tpu as pltpu
from jax.sharding import PartitionSpec as P

MESH = pl.DeviceIdType.MESH
F32 = jnp.float32
BF16 = jnp.bfloat16
NT = (((1,), (1,)), ((), ()))
NN = (((1,), (0,)), ((), ()))

ROWS = 75
BAND = 80
OWN = 8
NAO = 1200
DEPTH = 1280
COLS = 100
KROWS = 50
PAIRS = 64
SENT = 42
SLOT = 48


def split(v):
    hi = v.astype(BF16)
    return hi, (v - hi.astype(F32)).astype(BF16)


def widen(v):
    return jnp.concatenate([v, jnp.zeros((v.shape[0], DEPTH - NAO), F32)], axis=1)


def dot3(ah, al, bh, bl, dims):
    dot = functools.partial(lax.dot_general, dimension_numbers=dims, preferred_element_type=F32)
    return dot(ah, bh) + (dot(ah, bl) + dot(al, bh))


def kernel(x_ref, ct_ref, o, xbuf, cbuf, th, tl, fh, fl, sent, sentl, got, gotl, ah, al, product, m, xr, whole, n_,
           xsem, csem, s1, r1, l1, sx, rx, s2, r2, l2, ready):
    g = lax.axis_index("grp")
    w = lax.axis_index("wide")
    y, c = w // 2, lax.rem(w, 2)
    other = 1 - c
    barrier = pltpu.get_barrier_semaphore()

    loads = [pltpu.make_async_copy(ct_ref, cbuf, csem)]
    for p in range(OWN):
        loads.append(pltpu.make_async_copy(x_ref.at[:, p, :], xbuf.at[p], xsem.at[p]))
    for load in loads:
        load.start()

    src1 = g // 8
    src2 = y // 2

    def greet1(d, carry):
        gs = lax.rem(g + d, 16)

        @pl.when((d != 0) | (src1 != c))
        def _():
            pl.semaphore_signal(barrier, inc=1, device_id=(y * 2 + src1, gs), device_id_type=MESH)
        return carry

    lax.fori_loop(0, 16, greet1, 0)
    def greet2(d, carry):
        @pl.when(d != w)
        def _():
            pl.semaphore_signal(barrier, inc=1, device_id=(d, g), device_id_type=MESH)
        return carry

    lax.fori_loop(0, 8, greet2, 0)

    loads[0].wait()
    lane = lax.broadcasted_iota(jnp.int32, (16, DEPTH), 1)
    row = lax.broadcasted_iota(jnp.int32, (16, DEPTH), 0)

    def flat(b, carry):
        at = pl.multiple_of(16 * b, 16)
        hi, lo = split(widen(cbuf[pl.ds(at, 16), :]))
        fh[pl.ds(at, 16), :] = hi
        fl[pl.ds(at, 16), :] = lo
        return carry

    lax.fori_loop(0, 50, flat, 0)
    fh[pl.ds(800, 112), :] = jnp.zeros((112, DEPTH), BF16)
    fl[pl.ds(800, 112), :] = jnp.zeros((112, DEPTH), BF16)

    for p in range(OWN):
        loads[1 + p].wait()
        for b in range(5):
            height = min(16, ROWS - 16 * b)
            value = widen(xbuf[p, pl.ds(16 * b, height), :])
            if height < 16:
                value = jnp.concatenate([value, jnp.zeros((16 - height, DEPTH), F32)], axis=0)
            local = row + 16 * b
            s = local + ROWS * g
            value = jnp.where(lane < s, value, jnp.where(lane == s, 0.5 * value, 0.0))
            if b == 4:
                value = jnp.where(local < ROWS, value, 0.0)
            hi, lo = split(value)
            th[pl.ds(BAND * p + 16 * b, 16), :] = hi
            tl[pl.ds(BAND * p + 16 * b, 16), :] = lo

    for n in range(4):
        got[n, pl.ds(NAO, DEPTH - NAO), :] = jnp.zeros((DEPTH - NAO, 128), F32)

    narrow = lax.broadcasted_iota(jnp.int32, (8, 128), 1) < 16

    def stage1(q, carry):
        c2, h = lax.rem(q, 2), q // 2
        base = pl.multiple_of(c2 * 400 + h * 256, 16)
        acc = dot3(th[...], tl[...], fh[pl.ds(base, 256), :], fl[pl.ds(base, 256), :], NT)
        sent[2 * q] = acc[:, :128]

        @pl.when(h == 0)
        def _():
            sent[2 * q + 1] = acc[:, 128:]

        @pl.when(h == 1)
        def _():
            for i in range(OWN):
                parts = [jnp.where(narrow, acc[BAND * i + 8 * b:BAND * i + 8 * b + 8, 128:], 0.0) for b in range(10)]
                first = parts[0]
                for b in range(1, 8):
                    first = first + pltpu.roll(parts[b], 16 * b, 1)
                sentl[c2, pl.ds(16 * i, 8), :] = first
                sentl[c2, pl.ds(16 * i + 8, 8), :] = parts[8] + pltpu.roll(parts[9], 16, 1)

        @pl.when(q == 0)
        def _():
            pl.semaphore_wait(barrier, 16 + 7 - jnp.where(src1 == c, 1, 0))

        wd = y * 2 + c2

        def put(src, dst, j, k, tile):
            @pl.when((j != g) | (c2 != c))
            def _():
                pltpu.make_async_remote_copy(
                    src_ref=src, dst_ref=dst, send_sem=s1.at[q, k], recv_sem=r1.at[tile, g],
                    device_id=(wd, j), device_id_type=MESH).start()

            @pl.when((j == g) & (c2 == c))
            def _():
                pltpu.make_async_copy(src, dst, l1).start()
                pltpu.make_async_copy(src, dst, l1).wait()

        def send(k, carry):
            i = lax.rem(jnp.where(h == 0, k // 2, k) + g, 8)
            e = jnp.where(h == 0, lax.rem(k, 2), 1 - k // 8)
            j = 8 * c + i
            tile = 2 * h + e

            @pl.when(tile < 3)
            def _():
                put(sent.at[2 * q + e, pl.ds(i * BAND, ROWS), :], got.at[tile, pl.ds(ROWS * g, ROWS), :], j, k, tile)

            @pl.when(tile == 3)
            def _():
                put(sentl.at[c2, pl.ds(16 * i, 16), :], gotl.at[pl.ds(16 * g, 16), :], j, k, tile)
            return carry

        lax.fori_loop(0, 16, send, 0)
        return carry

    lax.fori_loop(0, 4, stage1, 0)

    def pass_on(d, carry):
        @pl.when(d != w)
        def _():
            pl.semaphore_signal(ready, inc=1, device_id=(d, g), device_id_type=MESH)
        return carry

    lax.fori_loop(0, 8, pass_on, 0)

    for n in range(4):
        for v in range(8):
            m[n, pl.ds(128 * v + COLS, 128 - COLS), :] = jnp.zeros((128 - COLS, 128), F32)

    pair = 16 * y + g

    def arrive(*tiles):
        for tile in tiles:
            def one(gs, carry):
                @pl.when((gs != g) | (src1 != c))
                def _():
                    if tile < 3:
                        src, dst = sent.at[0, pl.ds(0, ROWS), :], got.at[tile, pl.ds(ROWS * gs, ROWS), :]
                    else:
                        src, dst = sentl.at[0, pl.ds(0, 16), :], gotl.at[pl.ds(16 * gs, 16), :]
                    pltpu.make_async_remote_copy(
                        src_ref=src, dst_ref=dst, send_sem=s1.at[0, 0], recv_sem=r1.at[tile, gs],
                        device_id=(w, g), device_id_type=MESH).wait_recv()
                return carry

            lax.fori_loop(0, 16, one, 0)

    def multiply(h):
        def halves(b, carry):
            at = pl.multiple_of(b * 128, 128)
            here = lax.broadcasted_iota(jnp.int32, (128, 128), 1)
            for e in range(2):
                n = 2 * h + e
                value = got[n, pl.ds(at, 128), :]
                if n:
                    before = got[n - 1, pl.ds(at, 128), :]
                    value = jnp.where(here < 28 * n, pltpu.roll(before, 28 * n, 1), pltpu.roll(value, 28 * n, 1))
                hi, lo = split(value)
                ah[pl.ds(at, 128), pl.ds(128 * e, 128)] = hi
                al[pl.ds(at, 128), pl.ds(128 * e, 128)] = lo
            return carry

        lax.fori_loop(0, DEPTH // 128, halves, 0)

        def rows_of(half, carry):
            side = lax.rem(half + other, 2)
            at = pl.multiple_of(side * 512, 512)
            mine = pl.ds(pl.multiple_of(side * 400, 16), 400)
            product[...] = dot3(fh[mine, :], fl[mine, :], ah[...], al[...], NN)
            for a in range(4):
                for e in range(2):
                    m[2 * h + e, pl.ds(at + 128 * a, COLS), :] = product[pl.ds(COLS * a, COLS), pl.ds(128 * e, 128)]

            @pl.when(half == 0)
            def _():
                for e in range(2):
                    pltpu.make_async_remote_copy(
                        src_ref=m.at[2 * h + e, pl.ds(at, 512), :], dst_ref=xr.at[2 * h + e],
                        send_sem=sx.at[2 * h + e], recv_sem=rx.at[2 * h + e],
                        device_id=(y * 2 + other, g), device_id_type=MESH).start()
            return carry

        lax.fori_loop(0, 2, rows_of, 0)

    def crossed(h):
        for n in (2 * h, 2 * h + 1):
            pltpu.make_async_remote_copy(
                src_ref=m.at[n, pl.ds(0, 512), :], dst_ref=xr.at[n], send_sem=sx.at[n], recv_sem=rx.at[n],
                device_id=(w, g), device_id_type=MESH).wait()

    main = lax.broadcasted_iota(jnp.int32, (8, 128), 1) < COLS

    def add(across, a, n):
        half = other if across else c
        at = pl.multiple_of((4 * half + a) * 128, 128)
        if across:
            back = xr[a, pl.ds(pl.multiple_of(n * 128, 128), 128), :]
        else:
            back = m[a, pl.ds(pl.multiple_of((4 * c + n) * 128, 128), 128), :]
        whole[...] = m[n, pl.ds(at, 128), :] + back.T
        for r in range(2):
            slot = 2 * (4 * half + a) + r
            rest = whole[pl.ds(KROWS * r + SENT, 8), :]
            for j in range(4):
                n_[n, slot, pl.ds(8 * j, 8), :] = jnp.where(
                    main, whole[pl.ds(KROWS * r + 8 * j, 8), :], pltpu.roll(rest, COLS - 25 * j, 1))
            n_[n, slot, pl.ds(32, SENT - 32), :] = whole[pl.ds(KROWS * r + 32, SENT - 32), :]

    def spread(half, a, n, r):
        v = 4 * half + a
        wd = 4 * c + n
        gd = 2 * v + r
        src = n_.at[n, gd, pl.ds(0, SENT), :]
        dst = o.at[pl.ds(pair * SLOT, SENT), :]

        @pl.when((gd != g) | (wd != w))
        def _():
            pltpu.make_async_remote_copy(
                src_ref=src, dst_ref=dst, send_sem=s2.at[n, gd], recv_sem=r2.at[pair],
                device_id=(wd, gd), device_id_type=MESH).start()

        @pl.when((gd == g) & (wd == w))
        def _():
            pltpu.make_async_copy(src, dst, l2).start()
            pltpu.make_async_copy(src, dst, l2).wait()

    arrive(0, 1)
    multiply(0)
    crossed(0)

    def quarter(t, carry):
        add(False, t // 2, lax.rem(t, 2))
        add(True, t // 2, lax.rem(t, 2))
        return carry

    lax.fori_loop(0, 4, quarter, 0)

    pl.semaphore_wait(ready, 7)
    arrive(3)
    for gs in range(16):
        for b in range(10):
            part = gotl[pl.ds(16 * gs + 8 * (b // 8), 8), :]
            if b % 8:
                part = pltpu.roll(part, 128 - 16 * (b % 8), 1)
            got[3, pl.ds(ROWS * gs + 8 * b, 8), :] = part
    arrive(2)
    multiply(1)
    z, x = g // 4, lax.rem(g, 4)

    def out(t, carry):
        k = lax.rem(t * 11, 64)
        zd = 2 * lax.rem(k // 32 + c, 2) + lax.rem(k // 16 + z, 2)
        xd = lax.rem(k // 4 + x, 4)
        n = lax.rem(k + y, 4)
        half, r = zd // 2, lax.rem(xd, 2)
        a = 2 * lax.rem(zd, 2) + xd // 2
        twin = 16 * (k // 16) + 4 * lax.rem(xd + 1 - 2 * r + 4 - x, 4) + lax.rem(k, 4)
        first = ((a > 1) | (n > 1)) & (t < lax.rem(twin * 35, 64))

        @pl.when(t == 3)
        def _():
            crossed(1)

        @pl.when(first & (half == c))
        def _():
            add(False, a, n)

        @pl.when(first & (half != c))
        def _():
            add(True, a, n)

        spread(half, a, n, r)
        return carry

    lax.fori_loop(0, 64, out, 0)

    def left1(k, carry):
        q, kk = k // 16, lax.rem(k, 16)
        j = 8 * c + lax.rem(jnp.where(q < 2, kk // 2, kk) + g, 8)
        last = (q >= 2) & (kk < 8)
        moved = (j != g) | (lax.rem(q, 2) != c)

        def gone(src):
            pltpu.make_async_remote_copy(
                src_ref=src, dst_ref=src, send_sem=s1.at[q, kk], recv_sem=r1.at[0, 0],
                device_id=(w, g), device_id_type=MESH).wait_send()

        @pl.when(moved & jnp.logical_not(last))
        def _():
            gone(sent.at[0, pl.ds(0, ROWS), :])

        @pl.when(moved & last)
        def _():
            gone(sentl.at[0, pl.ds(0, 16), :])
        return carry

    lax.fori_loop(0, 64, left1, 0)

    def left2(k, carry):
        n, gd = k // 16, lax.rem(k, 16)

        @pl.when((gd != g) | (4 * c + n != w))
        def _():
            pltpu.make_async_remote_copy(
                src_ref=n_.at[0, 0, pl.ds(0, SENT), :], dst_ref=o.at[pl.ds(0, SENT), :],
                send_sem=s2.at[n, gd], recv_sem=r2.at[0], device_id=(w, g), device_id_type=MESH).wait_send()
        return carry

    lax.fori_loop(0, 64, left2, 0)

    def landed(q, carry):
        @pl.when((q != pair) | (src2 != c))
        def _():
            pltpu.make_async_remote_copy(
                src_ref=n_.at[0, 0, pl.ds(0, SENT), :], dst_ref=o.at[pl.ds(q * SLOT, SENT), :],
                send_sem=s2.at[0, 0], recv_sem=r2.at[q], device_id=(w, g), device_id_type=MESH).wait_recv()
        return carry

    lax.fori_loop(0, PAIRS, landed, 0)


def arrange(o_ref, out_ref):
    def plain(k, carry):
        for b in range(PAIRS // 8):
            out_ref[k, pl.ds(8 * b, 8), :] = o_ref[pl.ds(8 * b * SLOT + k, 8, stride=SLOT), :][:, :COLS]
        return carry

    lax.fori_loop(0, SENT, plain, 0, unroll=6)
    lane = lax.broadcasted_iota(jnp.int32, (8, 128), 1)

    def parts(q, carry):
        for b in range(PAIRS // 8):
            value = jnp.zeros((8, 128), F32)
            for j in range(4):
                part = o_ref[pl.ds(8 * b * SLOT + 8 * j + q, 8, stride=SLOT), :]
                part = pltpu.roll(part, 28 + 25 * j, 1)
                value = part if j == 0 else jnp.where(lane >= 25 * j, part, value)
            out_ref[SENT + q, pl.ds(8 * b, 8), :] = value[:, :COLS]
        return carry

    lax.fori_loop(0, 8, parts, 0, unroll=2)


def on_device(integrals, coeffs):
    dma = pltpu.SemaphoreType.DMA
    blocks = pl.pallas_call(
        kernel,
        out_shape=jax.ShapeDtypeStruct(((PAIRS + 1) * SLOT, 128), F32),
        in_specs=[pl.BlockSpec(memory_space=pl.ANY)] * 2,
        out_specs=pl.BlockSpec(memory_space=pl.ANY),
        scratch_shapes=[
            pltpu.VMEM((OWN, ROWS, NAO), F32),
            pltpu.VMEM((800, NAO), F32),
            pltpu.VMEM((OWN * BAND, DEPTH), BF16),
            pltpu.VMEM((OWN * BAND, DEPTH), BF16),
            pltpu.VMEM((912, DEPTH), BF16),
            pltpu.VMEM((912, DEPTH), BF16),
            pltpu.VMEM((8, OWN * BAND, 128), F32),
            pltpu.VMEM((2, OWN * 16, 128), F32),
            pltpu.VMEM((4, DEPTH, 128), F32),
            pltpu.VMEM((256, 128), F32),
            pltpu.VMEM((DEPTH, 256), BF16),
            pltpu.VMEM((DEPTH, 256), BF16),
            pltpu.VMEM((400, 256), F32),
            pltpu.VMEM((4, 1024, 128), F32),
            pltpu.VMEM((4, 512, 128), F32),
            pltpu.VMEM((128, 128), F32),
            pltpu.VMEM((4, 16, SLOT, 128), F32),
            dma((OWN,)), dma,
            dma((4, 16)), dma((4, 16)), dma,
            dma((4,)), dma((4,)),
            dma((4, 16)), dma((PAIRS,)), dma, pltpu.SemaphoreType.REGULAR,
        ],
        compiler_params=pltpu.CompilerParams(
            collective_id=0, has_side_effects=True, vmem_limit_bytes=51 * 2**20),
    )(integrals, coeffs.T)
    slab = pl.pallas_call(
        arrange,
        out_shape=jax.ShapeDtypeStruct((KROWS, PAIRS, COLS), F32),
        in_specs=[pl.BlockSpec(memory_space=pltpu.VMEM)],
        out_specs=pl.BlockSpec(memory_space=pltpu.VMEM),
        compiler_params=pltpu.CompilerParams(vmem_limit_bytes=16 * 2**20),
    )(blocks)
    return jnp.transpose(slab, (0, 2, 1))


def solution(mesh):
    return jax.shard_map(
        on_device,
        mesh=mesh,
        in_specs=(P("grp", "wide", None), P()),
        out_specs=P("grp", "wide", None),
        check_vma=False,
    )
```

```python
import functools

import jax
import jax.numpy as jnp
from jax import lax
from jax.experimental import pallas as pl
from jax.experimental.pallas import tpu as pltpu
from jax.sharding import PartitionSpec as P

MESH = pl.DeviceIdType.MESH
F32 = jnp.float32
BF16 = jnp.bfloat16
NT = (((1,), (1,)), ((), ()))
NN = (((1,), (0,)), ((), ()))

ROWS = 75
BAND = 80
OWN = 8
NAO = 1200
DEPTH = 1280
COLS = 100
KROWS = 50
PAIRS = 64
SENT = 42
SLOT = 48


def split(v):
    hi = v.astype(BF16)
    return hi, (v - hi.astype(F32)).astype(BF16)


def widen(v):
    return jnp.concatenate([v, jnp.zeros((v.shape[0], DEPTH - NAO), F32)], axis=1)


def dot3(ah, al, bh, bl, dims):
    dot = functools.partial(lax.dot_general, dimension_numbers=dims, preferred_element_type=F32)
    return dot(ah, bh) + (dot(ah, bl) + dot(al, bh))


def kernel(x_ref, ct_ref, o, xbuf, cbuf, th, tl, fh, fl, sent, sentl, got, gotl, ah, al, product, m, xr, whole, n_,
           xsem, csem, s1, r1, l1, sx, rx, s2, r2, l2, ready):
    g = lax.axis_index("grp")
    w = lax.axis_index("wide")
    y, c = w // 2, lax.rem(w, 2)
    other = 1 - c
    barrier = pltpu.get_barrier_semaphore()

    loads = [pltpu.make_async_copy(ct_ref, cbuf, csem)]
    for p in range(OWN):
        loads.append(pltpu.make_async_copy(x_ref.at[:, p, :], xbuf.at[p], xsem.at[p]))
    for load in loads:
        load.start()

    src1 = g // 8
    src2 = y // 2

    def greet1(d, carry):
        gs = lax.rem(g + d, 16)

        @pl.when((d != 0) | (src1 != c))
        def _():
            pl.semaphore_signal(barrier, inc=1, device_id=(y * 2 + src1, gs), device_id_type=MESH)
        return carry

    lax.fori_loop(0, 16, greet1, 0)
    def greet2(d, carry):
        @pl.when(d != w)
        def _():
            pl.semaphore_signal(barrier, inc=1, device_id=(d, g), device_id_type=MESH)
        return carry

    lax.fori_loop(0, 8, greet2, 0)

    loads[0].wait()
    lane = lax.broadcasted_iota(jnp.int32, (16, DEPTH), 1)
    row = lax.broadcasted_iota(jnp.int32, (16, DEPTH), 0)

    fh[pl.ds(800, 112), :] = jnp.zeros((112, DEPTH), BF16)
    fl[pl.ds(800, 112), :] = jnp.zeros((112, DEPTH), BF16)

    for p in range(OWN):
        loads[1 + p].wait()
        for b in range(5):
            height = min(16, ROWS - 16 * b)
            value = widen(xbuf[p, pl.ds(16 * b, height), :])
            if height < 16:
                value = jnp.concatenate([value, jnp.zeros((16 - height, DEPTH), F32)], axis=0)
            local = row + 16 * b
            s = local + ROWS * g
            value = jnp.where(lane < s, value, jnp.where(lane == s, 0.5 * value, 0.0))
            if b == 4:
                value = jnp.where(local < ROWS, value, 0.0)
            hi, lo = split(value)
            th[pl.ds(BAND * p + 16 * b, 16), :] = hi
            tl[pl.ds(BAND * p + 16 * b, 16), :] = lo

    for n in range(4):
        got[n, pl.ds(NAO, DEPTH - NAO), :] = jnp.zeros((DEPTH - NAO, 128), F32)

    narrow = lax.broadcasted_iota(jnp.int32, (8, 128), 1) < 16

    def stage1(q, carry):
        c2, h = lax.rem(q, 2), q // 2
        base = pl.multiple_of(c2 * 400 + h * 256, 16)

        def flat(b, carry):
            at = pl.multiple_of(base + 16 * b, 16)
            hi, lo = split(widen(cbuf[pl.ds(at, 16), :]))
            fh[pl.ds(at, 16), :] = hi
            fl[pl.ds(at, 16), :] = lo
            return carry

        lax.fori_loop(0, jnp.where(h == 0, 16, 9), flat, 0)
        acc = dot3(th[...], tl[...], fh[pl.ds(base, 256), :], fl[pl.ds(base, 256), :], NT)
        sent[2 * q] = acc[:, :128]

        @pl.when(h == 0)
        def _():
            sent[2 * q + 1] = acc[:, 128:]

        @pl.when(h == 1)
        def _():
            for i in range(OWN):
                parts = [jnp.where(narrow, acc[BAND * i + 8 * b:BAND * i + 8 * b + 8, 128:], 0.0) for b in range(10)]
                first = parts[0]
                for b in range(1, 8):
                    first = first + pltpu.roll(parts[b], 16 * b, 1)
                sentl[c2, pl.ds(16 * i, 8), :] = first
                sentl[c2, pl.ds(16 * i + 8, 8), :] = parts[8] + pltpu.roll(parts[9], 16, 1)

        @pl.when(q == 0)
        def _():
            pl.semaphore_wait(barrier, 16 + 7 - jnp.where(src1 == c, 1, 0))

        wd = y * 2 + c2

        def put(src, dst, j, k, tile):
            @pl.when((j != g) | (c2 != c))
            def _():
                pltpu.make_async_remote_copy(
                    src_ref=src, dst_ref=dst, send_sem=s1.at[q, k], recv_sem=r1.at[tile, g],
                    device_id=(wd, j), device_id_type=MESH).start()

            @pl.when((j == g) & (c2 == c))
            def _():
                pltpu.make_async_copy(src, dst, l1).start()
                pltpu.make_async_copy(src, dst, l1).wait()

        def send(k, carry):
            i = lax.rem(jnp.where(h == 0, k // 2, k) + g, 8)
            e = jnp.where(h == 0, lax.rem(k, 2), 1 - k // 8)
            j = 8 * c + i
            tile = 2 * h + e

            @pl.when(tile < 3)
            def _():
                put(sent.at[2 * q + e, pl.ds(i * BAND, ROWS), :], got.at[tile, pl.ds(ROWS * g, ROWS), :], j, k, tile)

            @pl.when(tile == 3)
            def _():
                put(sentl.at[c2, pl.ds(16 * i, 16), :], gotl.at[pl.ds(16 * g, 16), :], j, k, tile)
            return carry

        lax.fori_loop(0, 16, send, 0)
        return carry

    lax.fori_loop(0, 4, stage1, 0)

    def pass_on(d, carry):
        @pl.when(d != w)
        def _():
            pl.semaphore_signal(ready, inc=1, device_id=(d, g), device_id_type=MESH)
        return carry

    lax.fori_loop(0, 8, pass_on, 0)

    for n in range(4):
        for v in range(8):
            m[n, pl.ds(128 * v + COLS, 128 - COLS), :] = jnp.zeros((128 - COLS, 128), F32)

    pair = 16 * y + g

    def arrive(*tiles):
        for tile in tiles:
            def one(gs, carry):
                @pl.when((gs != g) | (src1 != c))
                def _():
                    if tile < 3:
                        src, dst = sent.at[0, pl.ds(0, ROWS), :], got.at[tile, pl.ds(ROWS * gs, ROWS), :]
                    else:
                        src, dst = sentl.at[0, pl.ds(0, 16), :], gotl.at[pl.ds(16 * gs, 16), :]
                    pltpu.make_async_remote_copy(
                        src_ref=src, dst_ref=dst, send_sem=s1.at[0, 0], recv_sem=r1.at[tile, gs],
                        device_id=(w, g), device_id_type=MESH).wait_recv()
                return carry

            lax.fori_loop(0, 16, one, 0)

    def multiply(h):
        def halves(b, carry):
            at = pl.multiple_of(b * 128, 128)
            here = lax.broadcasted_iota(jnp.int32, (128, 128), 1)
            for e in range(2):
                n = 2 * h + e
                value = got[n, pl.ds(at, 128), :]
                if n:
                    before = got[n - 1, pl.ds(at, 128), :]
                    value = jnp.where(here < 28 * n, pltpu.roll(before, 28 * n, 1), pltpu.roll(value, 28 * n, 1))
                hi, lo = split(value)
                ah[pl.ds(at, 128), pl.ds(128 * e, 128)] = hi
                al[pl.ds(at, 128), pl.ds(128 * e, 128)] = lo
            return carry

        lax.fori_loop(0, DEPTH // 128, halves, 0)

        def rows_of(half, carry):
            side = lax.rem(half + other, 2)
            at = pl.multiple_of(side * 512, 512)
            mine = pl.ds(pl.multiple_of(side * 400, 16), 400)
            product[...] = dot3(fh[mine, :], fl[mine, :], ah[...], al[...], NN)
            for a in range(4):
                for e in range(2):
                    m[2 * h + e, pl.ds(at + 128 * a, COLS), :] = product[pl.ds(COLS * a, COLS), pl.ds(128 * e, 128)]

            @pl.when(half == 0)
            def _():
                for e in range(2):
                    pltpu.make_async_remote_copy(
                        src_ref=m.at[2 * h + e, pl.ds(at, 512), :], dst_ref=xr.at[2 * h + e],
                        send_sem=sx.at[2 * h + e], recv_sem=rx.at[2 * h + e],
                        device_id=(y * 2 + other, g), device_id_type=MESH).start()
            return carry

        lax.fori_loop(0, 2, rows_of, 0)

    def crossed(h):
        for n in (2 * h, 2 * h + 1):
            pltpu.make_async_remote_copy(
                src_ref=m.at[n, pl.ds(0, 512), :], dst_ref=xr.at[n], send_sem=sx.at[n], recv_sem=rx.at[n],
                device_id=(w, g), device_id_type=MESH).wait()

    main = lax.broadcasted_iota(jnp.int32, (8, 128), 1) < COLS

    def add(across, a, n):
        half = other if across else c
        at = pl.multiple_of((4 * half + a) * 128, 128)
        if across:
            back = xr[a, pl.ds(pl.multiple_of(n * 128, 128), 128), :]
        else:
            back = m[a, pl.ds(pl.multiple_of((4 * c + n) * 128, 128), 128), :]
        whole[...] = m[n, pl.ds(at, 128), :] + back.T
        for r in range(2):
            slot = 2 * (4 * half + a) + r
            rest = whole[pl.ds(KROWS * r + SENT, 8), :]
            for j in range(4):
                n_[n, slot, pl.ds(8 * j, 8), :] = jnp.where(
                    main, whole[pl.ds(KROWS * r + 8 * j, 8), :], pltpu.roll(rest, COLS - 25 * j, 1))
            n_[n, slot, pl.ds(32, SENT - 32), :] = whole[pl.ds(KROWS * r + 32, SENT - 32), :]

    def spread(half, a, n, r):
        v = 4 * half + a
        wd = 4 * c + n
        gd = 2 * v + r
        src = n_.at[n, gd, pl.ds(0, SENT), :]
        dst = o.at[pl.ds(pair * SLOT, SENT), :]

        @pl.when((gd != g) | (wd != w))
        def _():
            pltpu.make_async_remote_copy(
                src_ref=src, dst_ref=dst, send_sem=s2.at[n, gd], recv_sem=r2.at[pair],
                device_id=(wd, gd), device_id_type=MESH).start()

        @pl.when((gd == g) & (wd == w))
        def _():
            pltpu.make_async_copy(src, dst, l2).start()
            pltpu.make_async_copy(src, dst, l2).wait()

    arrive(0, 1)
    multiply(0)
    crossed(0)

    def quarter(t, carry):
        add(False, t // 2, lax.rem(t, 2))
        add(True, t // 2, lax.rem(t, 2))
        return carry

    lax.fori_loop(0, 4, quarter, 0)

    pl.semaphore_wait(ready, 7)
    arrive(3)
    for gs in range(16):
        for b in range(10):
            part = gotl[pl.ds(16 * gs + 8 * (b // 8), 8), :]
            if b % 8:
                part = pltpu.roll(part, 128 - 16 * (b % 8), 1)
            got[3, pl.ds(ROWS * gs + 8 * b, 8), :] = part
    arrive(2)
    multiply(1)
    z, x = g // 4, lax.rem(g, 4)

    def out(t, carry):
        k = lax.rem(t * 11, 64)
        zd = 2 * lax.rem(k // 32 + c, 2) + lax.rem(k // 16 + z, 2)
        xd = lax.rem(k // 4 + x, 4)
        n = lax.rem(k + y, 4)
        half, r = zd // 2, lax.rem(xd, 2)
        a = 2 * lax.rem(zd, 2) + xd // 2
        twin = 16 * (k // 16) + 4 * lax.rem(xd + 1 - 2 * r + 4 - x, 4) + lax.rem(k, 4)
        first = ((a > 1) | (n > 1)) & (t < lax.rem(twin * 35, 64))

        @pl.when(t == 3)
        def _():
            crossed(1)

        @pl.when(first & (half == c))
        def _():
            add(False, a, n)

        @pl.when(first & (half != c))
        def _():
            add(True, a, n)

        spread(half, a, n, r)
        return carry

    lax.fori_loop(0, 64, out, 0)

    def left1(k, carry):
        q, kk = k // 16, lax.rem(k, 16)
        j = 8 * c + lax.rem(jnp.where(q < 2, kk // 2, kk) + g, 8)
        last = (q >= 2) & (kk < 8)
        moved = (j != g) | (lax.rem(q, 2) != c)

        def gone(src):
            pltpu.make_async_remote_copy(
                src_ref=src, dst_ref=src, send_sem=s1.at[q, kk], recv_sem=r1.at[0, 0],
                device_id=(w, g), device_id_type=MESH).wait_send()

        @pl.when(moved & jnp.logical_not(last))
        def _():
            gone(sent.at[0, pl.ds(0, ROWS), :])

        @pl.when(moved & last)
        def _():
            gone(sentl.at[0, pl.ds(0, 16), :])
        return carry

    lax.fori_loop(0, 64, left1, 0)

    def left2(k, carry):
        n, gd = k // 16, lax.rem(k, 16)

        @pl.when((gd != g) | (4 * c + n != w))
        def _():
            pltpu.make_async_remote_copy(
                src_ref=n_.at[0, 0, pl.ds(0, SENT), :], dst_ref=o.at[pl.ds(0, SENT), :],
                send_sem=s2.at[n, gd], recv_sem=r2.at[0], device_id=(w, g), device_id_type=MESH).wait_send()
        return carry

    lax.fori_loop(0, 64, left2, 0)

    def landed(q, carry):
        @pl.when((q != pair) | (src2 != c))
        def _():
            pltpu.make_async_remote_copy(
                src_ref=n_.at[0, 0, pl.ds(0, SENT), :], dst_ref=o.at[pl.ds(q * SLOT, SENT), :],
                send_sem=s2.at[0, 0], recv_sem=r2.at[q], device_id=(w, g), device_id_type=MESH).wait_recv()
        return carry

    lax.fori_loop(0, PAIRS, landed, 0)


def arrange(o_ref, out_ref, ready, sems):
    lane = lax.broadcasted_iota(jnp.int32, (8, 128), 1)

    def plain(k, carry):
        for b in range(PAIRS // 8):
            ready[k, pl.ds(8 * b, 8), :] = o_ref[pl.ds(8 * b * SLOT + k, 8, stride=SLOT), :][:, :COLS]
        return carry

    def parts(q, carry):
        for b in range(PAIRS // 8):
            value = jnp.zeros((8, 128), F32)
            for j in range(4):
                part = o_ref[pl.ds(8 * b * SLOT + 8 * j + q, 8, stride=SLOT), :]
                part = pltpu.roll(part, 28 + 25 * j, 1)
                value = part if j == 0 else jnp.where(lane >= 25 * j, part, value)
            ready[SENT + q, pl.ds(8 * b, 8), :] = value[:, :COLS]
        return carry

    copies = []
    for n, (start, rows) in enumerate(((SENT, 8), (0, 14), (14, 14), (28, 14))):
        if start == SENT:
            lax.fori_loop(0, 8, parts, 0, unroll=2)
        else:
            lax.fori_loop(start, start + rows, plain, 0, unroll=7)
        copies.append(pltpu.make_async_copy(ready.at[pl.ds(start, rows)], out_ref.at[pl.ds(start, rows)], sems.at[n]))
        copies[-1].start()
    for copy in copies:
        copy.wait()


def on_device(integrals, coeffs):
    dma = pltpu.SemaphoreType.DMA
    blocks = pl.pallas_call(
        kernel,
        out_shape=jax.ShapeDtypeStruct(((PAIRS + 1) * SLOT, 128), F32),
        in_specs=[pl.BlockSpec(memory_space=pl.ANY)] * 2,
        out_specs=pl.BlockSpec(memory_space=pl.ANY),
        scratch_shapes=[
            pltpu.VMEM((OWN, ROWS, NAO), F32),
            pltpu.VMEM((800, NAO), F32),
            pltpu.VMEM((OWN * BAND, DEPTH), BF16),
            pltpu.VMEM((OWN * BAND, DEPTH), BF16),
            pltpu.VMEM((912, DEPTH), BF16),
            pltpu.VMEM((912, DEPTH), BF16),
            pltpu.VMEM((8, OWN * BAND, 128), F32),
            pltpu.VMEM((2, OWN * 16, 128), F32),
            pltpu.VMEM((4, DEPTH, 128), F32),
            pltpu.VMEM((256, 128), F32),
            pltpu.VMEM((DEPTH, 256), BF16),
            pltpu.VMEM((DEPTH, 256), BF16),
            pltpu.VMEM((400, 256), F32),
            pltpu.VMEM((4, 1024, 128), F32),
            pltpu.VMEM((4, 512, 128), F32),
            pltpu.VMEM((128, 128), F32),
            pltpu.VMEM((4, 16, SLOT, 128), F32),
            dma((OWN,)), dma,
            dma((4, 16)), dma((4, 16)), dma,
            dma((4,)), dma((4,)),
            dma((4, 16)), dma((PAIRS,)), dma, pltpu.SemaphoreType.REGULAR,
        ],
        compiler_params=pltpu.CompilerParams(
            collective_id=0, has_side_effects=True, vmem_limit_bytes=51 * 2**20),
    )(integrals, coeffs.T)
    slab = pl.pallas_call(
        arrange,
        out_shape=jax.ShapeDtypeStruct((KROWS, PAIRS, COLS), F32),
        in_specs=[pl.BlockSpec(memory_space=pltpu.VMEM)],
        out_specs=pl.BlockSpec(memory_space=pl.ANY),
        scratch_shapes=[pltpu.VMEM((KROWS, PAIRS, COLS), F32), dma((4,))],
        compiler_params=pltpu.CompilerParams(vmem_limit_bytes=16 * 2**20),
    )(blocks)
    return jnp.transpose(slab, (0, 2, 1))


def solution(mesh):
    return jax.shard_map(
        on_device,
        mesh=mesh,
        in_specs=(P("grp", "wide", None), P()),
        out_specs=P("grp", "wide", None),
        check_vma=False,
    )
```

```python
import functools

import jax
import jax.numpy as jnp
from jax import lax
from jax.experimental import pallas as pl
from jax.experimental.pallas import tpu as pltpu
from jax.sharding import PartitionSpec as P

MESH = pl.DeviceIdType.MESH
F32 = jnp.float32
BF16 = jnp.bfloat16
NT = (((1,), (1,)), ((), ()))
NN = (((1,), (0,)), ((), ()))

ROWS = 75
BAND = 80
OWN = 8
NAO = 1200
DEPTH = 1280
COLS = 100
KROWS = 50
PAIRS = 64
SENT = 42
SLOT = 48


def split(v):
    hi = v.astype(BF16)
    return hi, (v - hi.astype(F32)).astype(BF16)


def widen(v):
    return jnp.concatenate([v, jnp.zeros((v.shape[0], DEPTH - NAO), F32)], axis=1)


def dot3(ah, al, bh, bl, dims):
    dot = functools.partial(lax.dot_general, dimension_numbers=dims, preferred_element_type=F32)
    return dot(ah, bh) + (dot(ah, bl) + dot(al, bh))


def kernel(x_ref, ct_ref, o, xbuf, cbuf, th, tl, fh, fl, sent, sentl, got, gotl, ah, al, product, m, xr, whole, n_,
           xsem, csem, s1, r1, l1, sx, rx, s2, r2, l2, ready):
    g = lax.axis_index("grp")
    w = lax.axis_index("wide")
    y, c = w // 2, lax.rem(w, 2)
    other = 1 - c
    barrier = pltpu.get_barrier_semaphore()

    loads = [pltpu.make_async_copy(ct_ref, cbuf, csem)]
    for p in range(OWN):
        loads.append(pltpu.make_async_copy(x_ref.at[:, p, :], xbuf.at[p], xsem.at[p]))
    for load in loads:
        load.start()

    src1 = g // 8
    src2 = y // 2

    def greet1(d, carry):
        gs = lax.rem(g + d, 16)

        @pl.when((d != 0) | (src1 != c))
        def _():
            pl.semaphore_signal(barrier, inc=1, device_id=(y * 2 + src1, gs), device_id_type=MESH)
        return carry

    lax.fori_loop(0, 16, greet1, 0)
    def greet2(d, carry):
        @pl.when(d != w)
        def _():
            pl.semaphore_signal(barrier, inc=1, device_id=(d, g), device_id_type=MESH)
        return carry

    lax.fori_loop(0, 8, greet2, 0)

    loads[0].wait()
    lane = lax.broadcasted_iota(jnp.int32, (16, DEPTH), 1)
    row = lax.broadcasted_iota(jnp.int32, (16, DEPTH), 0)

    fh[pl.ds(800, 112), :] = jnp.zeros((112, DEPTH), BF16)
    fl[pl.ds(800, 112), :] = jnp.zeros((112, DEPTH), BF16)

    for p in range(OWN):
        loads[1 + p].wait()
        for b in range(5):
            height = min(16, ROWS - 16 * b)
            value = widen(xbuf[p, pl.ds(16 * b, height), :])
            if height < 16:
                value = jnp.concatenate([value, jnp.zeros((16 - height, DEPTH), F32)], axis=0)
            local = row + 16 * b
            s = local + ROWS * g
            value = jnp.where(lane < s, value, jnp.where(lane == s, 0.5 * value, 0.0))
            if b == 4:
                value = jnp.where(local < ROWS, value, 0.0)
            hi, lo = split(value)
            th[pl.ds(BAND * p + 16 * b, 16), :] = hi
            tl[pl.ds(BAND * p + 16 * b, 16), :] = lo

    for n in range(4):
        got[n, pl.ds(NAO, DEPTH - NAO), :] = jnp.zeros((DEPTH - NAO, 128), F32)

    narrow = lax.broadcasted_iota(jnp.int32, (8, 128), 1) < 16

    def stage1(q, carry):
        c2, h = lax.rem(q, 2), q // 2
        base = pl.multiple_of(c2 * 400 + h * 256, 16)

        def flat(b, carry):
            at = pl.multiple_of(base + 16 * b, 16)
            hi, lo = split(widen(cbuf[pl.ds(at, 16), :]))
            fh[pl.ds(at, 16), :] = hi
            fl[pl.ds(at, 16), :] = lo
            return carry

        lax.fori_loop(0, jnp.where(h == 0, 16, 9), flat, 0)
        acc = dot3(th[...], tl[...], fh[pl.ds(base, 256), :], fl[pl.ds(base, 256), :], NT)
        sent[2 * q] = acc[:, :128]

        @pl.when(h == 0)
        def _():
            sent[2 * q + 1] = acc[:, 128:]

        @pl.when(h == 1)
        def _():
            for i in range(OWN):
                parts = [jnp.where(narrow, acc[BAND * i + 8 * b:BAND * i + 8 * b + 8, 128:], 0.0) for b in range(10)]
                first = parts[0]
                for b in range(1, 8):
                    first = first + pltpu.roll(parts[b], 16 * b, 1)
                sentl[c2, pl.ds(16 * i, 8), :] = first
                sentl[c2, pl.ds(16 * i + 8, 8), :] = parts[8] + pltpu.roll(parts[9], 16, 1)

        @pl.when(q == 0)
        def _():
            pl.semaphore_wait(barrier, 16 + 7 - jnp.where(src1 == c, 1, 0))

        wd = y * 2 + c2

        def put(src, dst, j, k, tile):
            @pl.when((j != g) | (c2 != c))
            def _():
                pltpu.make_async_remote_copy(
                    src_ref=src, dst_ref=dst, send_sem=s1.at[q, k], recv_sem=r1.at[tile, g],
                    device_id=(wd, j), device_id_type=MESH).start()

            @pl.when((j == g) & (c2 == c))
            def _():
                pltpu.make_async_copy(src, dst, l1).start()
                pltpu.make_async_copy(src, dst, l1).wait()

        def send(k, carry):
            i = lax.rem(k + g, 8)
            e = 1 - k // 8
            j = 8 * c + i
            tile = 2 * h + e

            @pl.when(tile < 3)
            def _():
                put(sent.at[2 * q + e, pl.ds(i * BAND, ROWS), :], got.at[tile, pl.ds(ROWS * g, ROWS), :], j, k, tile)

            @pl.when(tile == 3)
            def _():
                put(sentl.at[c2, pl.ds(16 * i, 16), :], gotl.at[pl.ds(16 * g, 16), :], j, k, tile)
            return carry

        lax.fori_loop(0, 16, send, 0)
        return carry

    lax.fori_loop(0, 4, stage1, 0)

    def pass_on(d, carry):
        @pl.when(d != w)
        def _():
            pl.semaphore_signal(ready, inc=1, device_id=(d, g), device_id_type=MESH)
        return carry

    lax.fori_loop(0, 8, pass_on, 0)

    for n in range(4):
        for v in range(8):
            m[n, pl.ds(128 * v + COLS, 128 - COLS), :] = jnp.zeros((128 - COLS, 128), F32)

    pair = 16 * y + g

    def arrive(*tiles):
        for tile in tiles:
            def one(gs, carry):
                @pl.when((gs != g) | (src1 != c))
                def _():
                    if tile < 3:
                        src, dst = sent.at[0, pl.ds(0, ROWS), :], got.at[tile, pl.ds(ROWS * gs, ROWS), :]
                    else:
                        src, dst = sentl.at[0, pl.ds(0, 16), :], gotl.at[pl.ds(16 * gs, 16), :]
                    pltpu.make_async_remote_copy(
                        src_ref=src, dst_ref=dst, send_sem=s1.at[0, 0], recv_sem=r1.at[tile, gs],
                        device_id=(w, g), device_id_type=MESH).wait_recv()
                return carry

            lax.fori_loop(0, 16, one, 0)

    def multiply(h):
        def halves(b, carry):
            at = pl.multiple_of(b * 128, 128)
            here = lax.broadcasted_iota(jnp.int32, (128, 128), 1)
            for e in range(2):
                n = 2 * h + e
                value = got[n, pl.ds(at, 128), :]
                if n:
                    before = got[n - 1, pl.ds(at, 128), :]
                    value = jnp.where(here < 28 * n, pltpu.roll(before, 28 * n, 1), pltpu.roll(value, 28 * n, 1))
                hi, lo = split(value)
                ah[pl.ds(at, 128), pl.ds(128 * e, 128)] = hi
                al[pl.ds(at, 128), pl.ds(128 * e, 128)] = lo
            return carry

        lax.fori_loop(0, DEPTH // 128, halves, 0)

        def rows_of(half, carry):
            side = lax.rem(half + other, 2)
            at = pl.multiple_of(side * 512, 512)
            mine = pl.ds(pl.multiple_of(side * 400, 16), 400)
            product[...] = dot3(fh[mine, :], fl[mine, :], ah[...], al[...], NN)
            for a in range(4):
                for e in range(2):
                    m[2 * h + e, pl.ds(at + 128 * a, COLS), :] = product[pl.ds(COLS * a, COLS), pl.ds(128 * e, 128)]

            @pl.when(half == 0)
            def _():
                for e in range(2):
                    pltpu.make_async_remote_copy(
                        src_ref=m.at[2 * h + e, pl.ds(at, 512), :], dst_ref=xr.at[2 * h + e],
                        send_sem=sx.at[2 * h + e], recv_sem=rx.at[2 * h + e],
                        device_id=(y * 2 + other, g), device_id_type=MESH).start()
            return carry

        lax.fori_loop(0, 2, rows_of, 0)

    def crossed(h):
        for n in (2 * h, 2 * h + 1):
            pltpu.make_async_remote_copy(
                src_ref=m.at[n, pl.ds(0, 512), :], dst_ref=xr.at[n], send_sem=sx.at[n], recv_sem=rx.at[n],
                device_id=(w, g), device_id_type=MESH).wait()

    main = lax.broadcasted_iota(jnp.int32, (8, 128), 1) < COLS

    def add(across, a, n):
        half = other if across else c
        at = pl.multiple_of((4 * half + a) * 128, 128)
        if across:
            back = xr[a, pl.ds(pl.multiple_of(n * 128, 128), 128), :]
        else:
            back = m[a, pl.ds(pl.multiple_of((4 * c + n) * 128, 128), 128), :]
        whole[...] = m[n, pl.ds(at, 128), :] + back.T
        for r in range(2):
            slot = 2 * (4 * half + a) + r
            rest = whole[pl.ds(KROWS * r + SENT, 8), :]
            for j in range(4):
                n_[n, slot, pl.ds(8 * j, 8), :] = jnp.where(
                    main, whole[pl.ds(KROWS * r + 8 * j, 8), :], pltpu.roll(rest, COLS - 25 * j, 1))
            n_[n, slot, pl.ds(32, SENT - 32), :] = whole[pl.ds(KROWS * r + 32, SENT - 32), :]

    def spread(half, a, n, r):
        v = 4 * half + a
        wd = 4 * c + n
        gd = 2 * v + r
        src = n_.at[n, gd, pl.ds(0, SENT), :]
        dst = o.at[pl.ds(pair * SLOT, SENT), :]

        @pl.when((gd != g) | (wd != w))
        def _():
            pltpu.make_async_remote_copy(
                src_ref=src, dst_ref=dst, send_sem=s2.at[n, gd], recv_sem=r2.at[pair],
                device_id=(wd, gd), device_id_type=MESH).start()

        @pl.when((gd == g) & (wd == w))
        def _():
            pltpu.make_async_copy(src, dst, l2).start()
            pltpu.make_async_copy(src, dst, l2).wait()

    arrive(0, 1)
    multiply(0)
    crossed(0)

    def quarter(t, carry):
        add(False, t // 2, lax.rem(t, 2))
        add(True, t // 2, lax.rem(t, 2))
        return carry

    lax.fori_loop(0, 4, quarter, 0)

    pl.semaphore_wait(ready, 7)
    arrive(3)
    for gs in range(16):
        for b in range(10):
            part = gotl[pl.ds(16 * gs + 8 * (b // 8), 8), :]
            if b % 8:
                part = pltpu.roll(part, 128 - 16 * (b % 8), 1)
            got[3, pl.ds(ROWS * gs + 8 * b, 8), :] = part
    arrive(2)
    multiply(1)
    z, x = g // 4, lax.rem(g, 4)

    def out(t, carry):
        k = lax.rem(t * 11, 64)
        zd = 2 * lax.rem(k // 32 + c, 2) + lax.rem(k // 16 + z, 2)
        xd = lax.rem(k // 4 + x, 4)
        n = lax.rem(k + y, 4)
        half, r = zd // 2, lax.rem(xd, 2)
        a = 2 * lax.rem(zd, 2) + xd // 2
        twin = 16 * (k // 16) + 4 * lax.rem(xd + 1 - 2 * r + 4 - x, 4) + lax.rem(k, 4)
        first = ((a > 1) | (n > 1)) & (t < lax.rem(twin * 35, 64))

        @pl.when(t == 3)
        def _():
            crossed(1)

        @pl.when(first & (half == c))
        def _():
            add(False, a, n)

        @pl.when(first & (half != c))
        def _():
            add(True, a, n)

        spread(half, a, n, r)
        return carry

    lax.fori_loop(0, 64, out, 0)

    def left1(k, carry):
        q, kk = k // 16, lax.rem(k, 16)
        j = 8 * c + lax.rem(kk + g, 8)
        last = (q >= 2) & (kk < 8)
        moved = (j != g) | (lax.rem(q, 2) != c)

        def gone(src):
            pltpu.make_async_remote_copy(
                src_ref=src, dst_ref=src, send_sem=s1.at[q, kk], recv_sem=r1.at[0, 0],
                device_id=(w, g), device_id_type=MESH).wait_send()

        @pl.when(moved & jnp.logical_not(last))
        def _():
            gone(sent.at[0, pl.ds(0, ROWS), :])

        @pl.when(moved & last)
        def _():
            gone(sentl.at[0, pl.ds(0, 16), :])
        return carry

    lax.fori_loop(0, 64, left1, 0)

    def left2(k, carry):
        n, gd = k // 16, lax.rem(k, 16)

        @pl.when((gd != g) | (4 * c + n != w))
        def _():
            pltpu.make_async_remote_copy(
                src_ref=n_.at[0, 0, pl.ds(0, SENT), :], dst_ref=o.at[pl.ds(0, SENT), :],
                send_sem=s2.at[n, gd], recv_sem=r2.at[0], device_id=(w, g), device_id_type=MESH).wait_send()
        return carry

    lax.fori_loop(0, 64, left2, 0)

    def landed(q, carry):
        @pl.when((q != pair) | (src2 != c))
        def _():
            pltpu.make_async_remote_copy(
                src_ref=n_.at[0, 0, pl.ds(0, SENT), :], dst_ref=o.at[pl.ds(q * SLOT, SENT), :],
                send_sem=s2.at[0, 0], recv_sem=r2.at[q], device_id=(w, g), device_id_type=MESH).wait_recv()
        return carry

    lax.fori_loop(0, PAIRS, landed, 0)


def arrange(o_ref, out_ref, ready, sems):
    lane = lax.broadcasted_iota(jnp.int32, (8, 128), 1)

    def plain(k, carry):
        for b in range(PAIRS // 8):
            ready[k, pl.ds(8 * b, 8), :] = o_ref[pl.ds(8 * b * SLOT + k, 8, stride=SLOT), :][:, :COLS]
        return carry

    def parts(q, carry):
        for b in range(PAIRS // 8):
            value = jnp.zeros((8, 128), F32)
            for j in range(4):
                part = o_ref[pl.ds(8 * b * SLOT + 8 * j + q, 8, stride=SLOT), :]
                part = pltpu.roll(part, 28 + 25 * j, 1)
                value = part if j == 0 else jnp.where(lane >= 25 * j, part, value)
            ready[SENT + q, pl.ds(8 * b, 8), :] = value[:, :COLS]
        return carry

    copies = []
    for n, (start, rows) in enumerate(((SENT, 8), (0, 14), (14, 14), (28, 14))):
        if start == SENT:
            lax.fori_loop(0, 8, parts, 0, unroll=2)
        else:
            lax.fori_loop(start, start + rows, plain, 0, unroll=7)
        copies.append(pltpu.make_async_copy(ready.at[pl.ds(start, rows)], out_ref.at[pl.ds(start, rows)], sems.at[n]))
        copies[-1].start()
    for copy in copies:
        copy.wait()


def on_device(integrals, coeffs):
    dma = pltpu.SemaphoreType.DMA
    blocks = pl.pallas_call(
        kernel,
        out_shape=jax.ShapeDtypeStruct(((PAIRS + 1) * SLOT, 128), F32),
        in_specs=[pl.BlockSpec(memory_space=pl.ANY)] * 2,
        out_specs=pl.BlockSpec(memory_space=pl.ANY),
        scratch_shapes=[
            pltpu.VMEM((OWN, ROWS, NAO), F32),
            pltpu.VMEM((800, NAO), F32),
            pltpu.VMEM((OWN * BAND, DEPTH), BF16),
            pltpu.VMEM((OWN * BAND, DEPTH), BF16),
            pltpu.VMEM((912, DEPTH), BF16),
            pltpu.VMEM((912, DEPTH), BF16),
            pltpu.VMEM((8, OWN * BAND, 128), F32),
            pltpu.VMEM((2, OWN * 16, 128), F32),
            pltpu.VMEM((4, DEPTH, 128), F32),
            pltpu.VMEM((256, 128), F32),
            pltpu.VMEM((DEPTH, 256), BF16),
            pltpu.VMEM((DEPTH, 256), BF16),
            pltpu.VMEM((400, 256), F32),
            pltpu.VMEM((4, 1024, 128), F32),
            pltpu.VMEM((4, 512, 128), F32),
            pltpu.VMEM((128, 128), F32),
            pltpu.VMEM((4, 16, SLOT, 128), F32),
            dma((OWN,)), dma,
            dma((4, 16)), dma((4, 16)), dma,
            dma((4,)), dma((4,)),
            dma((4, 16)), dma((PAIRS,)), dma, pltpu.SemaphoreType.REGULAR,
        ],
        compiler_params=pltpu.CompilerParams(
            collective_id=0, has_side_effects=True, vmem_limit_bytes=51 * 2**20),
    )(integrals, coeffs.T)
    slab = pl.pallas_call(
        arrange,
        out_shape=jax.ShapeDtypeStruct((KROWS, PAIRS, COLS), F32),
        in_specs=[pl.BlockSpec(memory_space=pltpu.VMEM)],
        out_specs=pl.BlockSpec(memory_space=pl.ANY),
        scratch_shapes=[pltpu.VMEM((KROWS, PAIRS, COLS), F32), dma((4,))],
        compiler_params=pltpu.CompilerParams(vmem_limit_bytes=16 * 2**20),
    )(blocks)
    return jnp.transpose(slab, (0, 2, 1))


def solution(mesh):
    return jax.shard_map(
        on_device,
        mesh=mesh,
        in_specs=(P("grp", "wide", None), P()),
        out_specs=P("grp", "wide", None),
        check_vma=False,
    )
```

```python
import functools

import jax
import jax.numpy as jnp
from jax import lax
from jax.experimental import pallas as pl
from jax.experimental.pallas import tpu as pltpu
from jax.sharding import PartitionSpec as P

MESH = pl.DeviceIdType.MESH
F32 = jnp.float32
BF16 = jnp.bfloat16
NT = (((1,), (1,)), ((), ()))
NN = (((1,), (0,)), ((), ()))

ROWS = 75
BAND = 80
OWN = 8
NAO = 1200
DEPTH = 1280
COLS = 100
KROWS = 50
PAIRS = 64
SENT = 42
SLOT = 48


def split(v):
    hi = v.astype(BF16)
    return hi, (v - hi.astype(F32)).astype(BF16)


def widen(v):
    return jnp.concatenate([v, jnp.zeros((v.shape[0], DEPTH - NAO), F32)], axis=1)


def dot3(ah, al, bh, bl, dims):
    dot = functools.partial(lax.dot_general, dimension_numbers=dims, preferred_element_type=F32)
    return dot(ah, bh) + (dot(ah, bl) + dot(al, bh))


def kernel(x_ref, ct_ref, o, xbuf, cbuf, th, tl, fh, fl, sent, sentl, got, gotl, ah, al, product, m, xr, whole, n_,
           xsem, csem, s1, r1, l1, sx, rx, s2, r2, l2, ready):
    g = lax.axis_index("grp")
    w = lax.axis_index("wide")
    y, c = w // 2, lax.rem(w, 2)
    other = 1 - c
    barrier = pltpu.get_barrier_semaphore()

    loads = [pltpu.make_async_copy(ct_ref, cbuf, csem)]
    for p in range(OWN):
        loads.append(pltpu.make_async_copy(x_ref.at[:, p, :], xbuf.at[p], xsem.at[p]))
    for load in loads:
        load.start()

    src1 = g // 8
    src2 = y // 2

    def greet1(d, carry):
        gs = lax.rem(g + d, 16)

        @pl.when((d != 0) | (src1 != c))
        def _():
            pl.semaphore_signal(barrier, inc=1, device_id=(y * 2 + src1, gs), device_id_type=MESH)
        return carry

    lax.fori_loop(0, 16, greet1, 0)
    def greet2(d, carry):
        @pl.when(d != w)
        def _():
            pl.semaphore_signal(barrier, inc=1, device_id=(d, g), device_id_type=MESH)
        return carry

    lax.fori_loop(0, 8, greet2, 0)

    loads[0].wait()
    lane = lax.broadcasted_iota(jnp.int32, (16, DEPTH), 1)
    row = lax.broadcasted_iota(jnp.int32, (16, DEPTH), 0)

    fh[pl.ds(800, 112), :] = jnp.zeros((112, DEPTH), BF16)
    fl[pl.ds(800, 112), :] = jnp.zeros((112, DEPTH), BF16)

    for p in range(OWN):
        loads[1 + p].wait()
        for b in range(5):
            height = min(16, ROWS - 16 * b)
            value = widen(xbuf[p, pl.ds(16 * b, height), :])
            if height < 16:
                value = jnp.concatenate([value, jnp.zeros((16 - height, DEPTH), F32)], axis=0)
            local = row + 16 * b
            s = local + ROWS * g
            value = jnp.where(lane < s, value, jnp.where(lane == s, 0.5 * value, 0.0))
            if b == 4:
                value = jnp.where(local < ROWS, value, 0.0)
            hi, lo = split(value)
            th[pl.ds(BAND * p + 16 * b, 16), :] = hi
            tl[pl.ds(BAND * p + 16 * b, 16), :] = lo

    for n in range(4):
        got[n, pl.ds(NAO, DEPTH - NAO), :] = jnp.zeros((DEPTH - NAO, 128), F32)

    narrow = lax.broadcasted_iota(jnp.int32, (8, 128), 1) < 16

    def stage1(q, carry):
        c2, h = lax.rem(q, 2), q // 2
        base = pl.multiple_of(c2 * 400 + h * 256, 16)

        def flat(b, carry):
            at = pl.multiple_of(base + 16 * b, 16)
            hi, lo = split(widen(cbuf[pl.ds(at, 16), :]))
            fh[pl.ds(at, 16), :] = hi
            fl[pl.ds(at, 16), :] = lo
            return carry

        lax.fori_loop(0, jnp.where(h == 0, 16, 9), flat, 0)
        acc = dot3(th[...], tl[...], fh[pl.ds(base, 256), :], fl[pl.ds(base, 256), :], NT)
        sent[2 * q] = acc[:, :128]

        @pl.when(h == 0)
        def _():
            sent[2 * q + 1] = acc[:, 128:]

        @pl.when(h == 1)
        def _():
            for i in range(OWN):
                parts = [jnp.where(narrow, acc[BAND * i + 8 * b:BAND * i + 8 * b + 8, 128:], 0.0) for b in range(10)]
                first = parts[0]
                for b in range(1, 8):
                    first = first + pltpu.roll(parts[b], 16 * b, 1)
                sentl[c2, pl.ds(16 * i, 8), :] = first
                sentl[c2, pl.ds(16 * i + 8, 8), :] = parts[8] + pltpu.roll(parts[9], 16, 1)

        @pl.when(q == 0)
        def _():
            pl.semaphore_wait(barrier, 16 + 7 - jnp.where(src1 == c, 1, 0))

        wd = y * 2 + c2

        def put(src, dst, j, k, tile):
            @pl.when((j != g) | (c2 != c))
            def _():
                pltpu.make_async_remote_copy(
                    src_ref=src, dst_ref=dst, send_sem=s1.at[q, k], recv_sem=r1.at[tile, g],
                    device_id=(wd, j), device_id_type=MESH).start()

            @pl.when((j == g) & (c2 == c))
            def _():
                pltpu.make_async_copy(src, dst, l1).start()
                pltpu.make_async_copy(src, dst, l1).wait()

        def send(k, carry):
            i = lax.rem(k + g, 8)
            e = 1 - k // 8
            j = 8 * c + i
            tile = 2 * h + e

            @pl.when(tile < 3)
            def _():
                put(sent.at[2 * q + e, pl.ds(i * BAND, ROWS), :], got.at[tile, pl.ds(ROWS * g, ROWS), :], j, k, tile)

            @pl.when(tile == 3)
            def _():
                put(sentl.at[c2, pl.ds(16 * i, 16), :], gotl.at[pl.ds(16 * g, 16), :], j, k, tile)
            return carry

        lax.fori_loop(0, 16, send, 0)
        return carry

    lax.fori_loop(0, 4, stage1, 0)

    def pass_on(d, carry):
        @pl.when(d != w)
        def _():
            pl.semaphore_signal(ready, inc=1, device_id=(d, g), device_id_type=MESH)
        return carry

    lax.fori_loop(0, 8, pass_on, 0)

    for n in range(4):
        for v in range(8):
            m[n, pl.ds(128 * v + COLS, 128 - COLS), :] = jnp.zeros((128 - COLS, 128), F32)

    pair = 16 * y + g

    def arrive(*tiles):
        for tile in tiles:
            def one(gs, carry):
                @pl.when((gs != g) | (src1 != c))
                def _():
                    if tile < 3:
                        src, dst = sent.at[0, pl.ds(0, ROWS), :], got.at[tile, pl.ds(ROWS * gs, ROWS), :]
                    else:
                        src, dst = sentl.at[0, pl.ds(0, 16), :], gotl.at[pl.ds(16 * gs, 16), :]
                    pltpu.make_async_remote_copy(
                        src_ref=src, dst_ref=dst, send_sem=s1.at[0, 0], recv_sem=r1.at[tile, gs],
                        device_id=(w, g), device_id_type=MESH).wait_recv()
                return carry

            lax.fori_loop(0, 16, one, 0)

    def multiply(h):
        def halves(b, carry):
            at = pl.multiple_of(b * 128, 128)
            here = lax.broadcasted_iota(jnp.int32, (128, 128), 1)
            for e in range(2):
                n = 2 * h + e
                value = got[n, pl.ds(at, 128), :]
                if n:
                    before = got[n - 1, pl.ds(at, 128), :]
                    value = jnp.where(here < 28 * n, pltpu.roll(before, 28 * n, 1), pltpu.roll(value, 28 * n, 1))
                hi, lo = split(value)
                ah[pl.ds(at, 128), pl.ds(128 * e, 128)] = hi
                al[pl.ds(at, 128), pl.ds(128 * e, 128)] = lo
            return carry

        lax.fori_loop(0, DEPTH // 128, halves, 0, unroll=5)

        def rows_of(half, carry):
            side = lax.rem(half + other, 2)
            at = pl.multiple_of(side * 512, 512)
            mine = pl.ds(pl.multiple_of(side * 400, 16), 400)
            product[...] = dot3(fh[mine, :], fl[mine, :], ah[...], al[...], NN)
            for a in range(4):
                for e in range(2):
                    m[2 * h + e, pl.ds(at + 128 * a, COLS), :] = product[pl.ds(COLS * a, COLS), pl.ds(128 * e, 128)]

            @pl.when(half == 0)
            def _():
                for e in range(2):
                    pltpu.make_async_remote_copy(
                        src_ref=m.at[2 * h + e, pl.ds(at, 512), :], dst_ref=xr.at[2 * h + e],
                        send_sem=sx.at[2 * h + e], recv_sem=rx.at[2 * h + e],
                        device_id=(y * 2 + other, g), device_id_type=MESH).start()
            return carry

        lax.fori_loop(0, 2, rows_of, 0)

    def crossed(h):
        for n in (2 * h, 2 * h + 1):
            pltpu.make_async_remote_copy(
                src_ref=m.at[n, pl.ds(0, 512), :], dst_ref=xr.at[n], send_sem=sx.at[n], recv_sem=rx.at[n],
                device_id=(w, g), device_id_type=MESH).wait()

    main = lax.broadcasted_iota(jnp.int32, (8, 128), 1) < COLS

    def add(across, a, n):
        half = other if across else c
        at = pl.multiple_of((4 * half + a) * 128, 128)
        if across:
            back = xr[a, pl.ds(pl.multiple_of(n * 128, 128), 128), :]
        else:
            back = m[a, pl.ds(pl.multiple_of((4 * c + n) * 128, 128), 128), :]
        whole[...] = m[n, pl.ds(at, 128), :] + back.T
        for r in range(2):
            slot = 2 * (4 * half + a) + r
            rest = whole[pl.ds(KROWS * r + SENT, 8), :]
            for j in range(4):
                n_[n, slot, pl.ds(8 * j, 8), :] = jnp.where(
                    main, whole[pl.ds(KROWS * r + 8 * j, 8), :], pltpu.roll(rest, COLS - 25 * j, 1))
            n_[n, slot, pl.ds(32, SENT - 32), :] = whole[pl.ds(KROWS * r + 32, SENT - 32), :]

    def spread(half, a, n, r):
        v = 4 * half + a
        wd = 4 * c + n
        gd = 2 * v + r
        src = n_.at[n, gd, pl.ds(0, SENT), :]
        dst = o.at[pl.ds(pair * SLOT, SENT), :]

        @pl.when((gd != g) | (wd != w))
        def _():
            pltpu.make_async_remote_copy(
                src_ref=src, dst_ref=dst, send_sem=s2.at[n, gd], recv_sem=r2.at[pair],
                device_id=(wd, gd), device_id_type=MESH).start()

        @pl.when((gd == g) & (wd == w))
        def _():
            pltpu.make_async_copy(src, dst, l2).start()
            pltpu.make_async_copy(src, dst, l2).wait()

    arrive(0, 1)
    multiply(0)
    crossed(0)

    def quarter(t, carry):
        add(False, t // 2, lax.rem(t, 2))
        add(True, t // 2, lax.rem(t, 2))
        return carry

    lax.fori_loop(0, 4, quarter, 0)

    pl.semaphore_wait(ready, 7)
    arrive(3)
    for gs in range(16):
        for b in range(10):
            part = gotl[pl.ds(16 * gs + 8 * (b // 8), 8), :]
            if b % 8:
                part = pltpu.roll(part, 128 - 16 * (b % 8), 1)
            got[3, pl.ds(ROWS * gs + 8 * b, 8), :] = part
    arrive(2)
    multiply(1)
    z, x = g // 4, lax.rem(g, 4)

    def out(t, carry):
        k = lax.rem(t * 11, 64)
        zd = 2 * lax.rem(k // 32 + c, 2) + lax.rem(k // 16 + z, 2)
        xd = lax.rem(k // 4 + x, 4)
        n = lax.rem(k + y, 4)
        half, r = zd // 2, lax.rem(xd, 2)
        a = 2 * lax.rem(zd, 2) + xd // 2
        twin = 16 * (k // 16) + 4 * lax.rem(xd + 1 - 2 * r + 4 - x, 4) + lax.rem(k, 4)
        first = ((a > 1) | (n > 1)) & (t < lax.rem(twin * 35, 64))

        @pl.when(t == 3)
        def _():
            crossed(1)

        @pl.when(first & (half == c))
        def _():
            add(False, a, n)

        @pl.when(first & (half != c))
        def _():
            add(True, a, n)

        spread(half, a, n, r)
        return carry

    lax.fori_loop(0, 64, out, 0)

    def left1(k, carry):
        q, kk = k // 16, lax.rem(k, 16)
        j = 8 * c + lax.rem(kk + g, 8)
        last = (q >= 2) & (kk < 8)
        moved = (j != g) | (lax.rem(q, 2) != c)

        def gone(src):
            pltpu.make_async_remote_copy(
                src_ref=src, dst_ref=src, send_sem=s1.at[q, kk], recv_sem=r1.at[0, 0],
                device_id=(w, g), device_id_type=MESH).wait_send()

        @pl.when(moved & jnp.logical_not(last))
        def _():
            gone(sent.at[0, pl.ds(0, ROWS), :])

        @pl.when(moved & last)
        def _():
            gone(sentl.at[0, pl.ds(0, 16), :])
        return carry

    lax.fori_loop(0, 64, left1, 0)

    def left2(k, carry):
        n, gd = k // 16, lax.rem(k, 16)

        @pl.when((gd != g) | (4 * c + n != w))
        def _():
            pltpu.make_async_remote_copy(
                src_ref=n_.at[0, 0, pl.ds(0, SENT), :], dst_ref=o.at[pl.ds(0, SENT), :],
                send_sem=s2.at[n, gd], recv_sem=r2.at[0], device_id=(w, g), device_id_type=MESH).wait_send()
        return carry

    lax.fori_loop(0, 64, left2, 0)

    def landed(q, carry):
        @pl.when((q != pair) | (src2 != c))
        def _():
            pltpu.make_async_remote_copy(
                src_ref=n_.at[0, 0, pl.ds(0, SENT), :], dst_ref=o.at[pl.ds(q * SLOT, SENT), :],
                send_sem=s2.at[0, 0], recv_sem=r2.at[q], device_id=(w, g), device_id_type=MESH).wait_recv()
        return carry

    lax.fori_loop(0, PAIRS, landed, 0)


def arrange(o_ref, out_ref, ready, sems):
    lane = lax.broadcasted_iota(jnp.int32, (8, 128), 1)

    def plain(k, carry):
        for b in range(PAIRS // 8):
            ready[k, pl.ds(8 * b, 8), :] = o_ref[pl.ds(8 * b * SLOT + k, 8, stride=SLOT), :][:, :COLS]
        return carry

    def parts(q, carry):
        for b in range(PAIRS // 8):
            value = jnp.zeros((8, 128), F32)
            for j in range(4):
                part = o_ref[pl.ds(8 * b * SLOT + 8 * j + q, 8, stride=SLOT), :]
                part = pltpu.roll(part, 28 + 25 * j, 1)
                value = part if j == 0 else jnp.where(lane >= 25 * j, part, value)
            ready[SENT + q, pl.ds(8 * b, 8), :] = value[:, :COLS]
        return carry

    copies = []
    for n, (start, rows) in enumerate(((SENT, 8), (0, 14), (14, 14), (28, 14))):
        if start == SENT:
            lax.fori_loop(0, 8, parts, 0, unroll=2)
        else:
            lax.fori_loop(start, start + rows, plain, 0, unroll=7)
        copies.append(pltpu.make_async_copy(ready.at[pl.ds(start, rows)], out_ref.at[pl.ds(start, rows)], sems.at[n]))
        copies[-1].start()
    for copy in copies:
        copy.wait()


def on_device(integrals, coeffs):
    dma = pltpu.SemaphoreType.DMA
    blocks = pl.pallas_call(
        kernel,
        out_shape=jax.ShapeDtypeStruct(((PAIRS + 1) * SLOT, 128), F32),
        in_specs=[pl.BlockSpec(memory_space=pl.ANY)] * 2,
        out_specs=pl.BlockSpec(memory_space=pl.ANY),
        scratch_shapes=[
            pltpu.VMEM((OWN, ROWS, NAO), F32),
            pltpu.VMEM((800, NAO), F32),
            pltpu.VMEM((OWN * BAND, DEPTH), BF16),
            pltpu.VMEM((OWN * BAND, DEPTH), BF16),
            pltpu.VMEM((912, DEPTH), BF16),
            pltpu.VMEM((912, DEPTH), BF16),
            pltpu.VMEM((8, OWN * BAND, 128), F32),
            pltpu.VMEM((2, OWN * 16, 128), F32),
            pltpu.VMEM((4, DEPTH, 128), F32),
            pltpu.VMEM((256, 128), F32),
            pltpu.VMEM((DEPTH, 256), BF16),
            pltpu.VMEM((DEPTH, 256), BF16),
            pltpu.VMEM((400, 256), F32),
            pltpu.VMEM((4, 1024, 128), F32),
            pltpu.VMEM((4, 512, 128), F32),
            pltpu.VMEM((128, 128), F32),
            pltpu.VMEM((4, 16, SLOT, 128), F32),
            dma((OWN,)), dma,
            dma((4, 16)), dma((4, 16)), dma,
            dma((4,)), dma((4,)),
            dma((4, 16)), dma((PAIRS,)), dma, pltpu.SemaphoreType.REGULAR,
        ],
        compiler_params=pltpu.CompilerParams(
            collective_id=0, has_side_effects=True, vmem_limit_bytes=51 * 2**20),
    )(integrals, coeffs.T)
    slab = pl.pallas_call(
        arrange,
        out_shape=jax.ShapeDtypeStruct((KROWS, PAIRS, COLS), F32),
        in_specs=[pl.BlockSpec(memory_space=pltpu.VMEM)],
        out_specs=pl.BlockSpec(memory_space=pl.ANY),
        scratch_shapes=[pltpu.VMEM((KROWS, PAIRS, COLS), F32), dma((4,))],
        compiler_params=pltpu.CompilerParams(vmem_limit_bytes=16 * 2**20),
    )(blocks)
    return jnp.transpose(slab, (0, 2, 1))


def solution(mesh):
    return jax.shard_map(
        on_device,
        mesh=mesh,
        in_specs=(P("grp", "wide", None), P()),
        out_specs=P("grp", "wide", None),
        check_vma=False,
    )
```

```python
import functools

import jax
import jax.numpy as jnp
from jax import lax
from jax.experimental import pallas as pl
from jax.experimental.pallas import tpu as pltpu
from jax.sharding import PartitionSpec as P

MESH = pl.DeviceIdType.MESH
F32 = jnp.float32
BF16 = jnp.bfloat16
NT = (((1,), (1,)), ((), ()))
NN = (((1,), (0,)), ((), ()))

ROWS = 75
BAND = 80
OWN = 8
NAO = 1200
DEPTH = 1280
COLS = 100
KROWS = 50
PAIRS = 64
SENT = 42
SLOT = 48


def split(v):
    hi = v.astype(BF16)
    return hi, (v - hi.astype(F32)).astype(BF16)


def widen(v):
    return jnp.concatenate([v, jnp.zeros((v.shape[0], DEPTH - NAO), F32)], axis=1)


def dot3(ah, al, bh, bl, dims):
    dot = functools.partial(lax.dot_general, dimension_numbers=dims, preferred_element_type=F32)
    return dot(ah, bh) + (dot(ah, bl) + dot(al, bh))


def kernel(x_ref, ct_ref, o, xbuf, cbuf, th, tl, fh, fl, sent, sentl, got, gotl, ah, al, product, m, xr, whole, n_,
           xsem, csem, s1, r1, l1, sx, rx, s2, r2, l2, ready):
    g = lax.axis_index("grp")
    w = lax.axis_index("wide")
    y, c = w // 2, lax.rem(w, 2)
    other = 1 - c
    barrier = pltpu.get_barrier_semaphore()

    loads = [pltpu.make_async_copy(ct_ref, cbuf, csem)]
    for p in range(OWN):
        loads.append(pltpu.make_async_copy(x_ref.at[:, p, :], xbuf.at[p], xsem.at[p]))
    for load in loads:
        load.start()

    src1 = g // 8
    src2 = y // 2

    def greet1(d, carry):
        gs = lax.rem(g + d, 16)

        @pl.when((d != 0) | (src1 != c))
        def _():
            pl.semaphore_signal(barrier, inc=1, device_id=(y * 2 + src1, gs), device_id_type=MESH)
        return carry

    lax.fori_loop(0, 16, greet1, 0)
    def greet2(d, carry):
        @pl.when(d != w)
        def _():
            pl.semaphore_signal(barrier, inc=1, device_id=(d, g), device_id_type=MESH)
        return carry

    lax.fori_loop(0, 8, greet2, 0)

    loads[0].wait()
    lane = lax.broadcasted_iota(jnp.int32, (16, DEPTH), 1)
    row = lax.broadcasted_iota(jnp.int32, (16, DEPTH), 0)

    fh[pl.ds(800, 112), :] = jnp.zeros((112, DEPTH), BF16)
    fl[pl.ds(800, 112), :] = jnp.zeros((112, DEPTH), BF16)

    for p in range(OWN):
        loads[1 + p].wait()
        for b in range(5):
            height = min(16, ROWS - 16 * b)
            value = widen(xbuf[p, pl.ds(16 * b, height), :])
            if height < 16:
                value = jnp.concatenate([value, jnp.zeros((16 - height, DEPTH), F32)], axis=0)
            local = row + 16 * b
            s = local + ROWS * g
            value = jnp.where(lane < s, value, jnp.where(lane == s, 0.5 * value, 0.0))
            if b == 4:
                value = jnp.where(local < ROWS, value, 0.0)
            hi, lo = split(value)
            th[pl.ds(BAND * p + 16 * b, 16), :] = hi
            tl[pl.ds(BAND * p + 16 * b, 16), :] = lo

    for n in range(4):
        got[n, pl.ds(NAO, DEPTH - NAO), :] = jnp.zeros((DEPTH - NAO, 128), F32)

    narrow = lax.broadcasted_iota(jnp.int32, (8, 128), 1) < 16

    def stage1(q, carry):
        c2, h = lax.rem(q, 2), q // 2
        base = pl.multiple_of(c2 * 400 + h * 256, 16)

        def flat(b, carry):
            at = pl.multiple_of(base + 16 * b, 16)
            hi, lo = split(widen(cbuf[pl.ds(at, 16), :]))
            fh[pl.ds(at, 16), :] = hi
            fl[pl.ds(at, 16), :] = lo
            return carry

        lax.fori_loop(0, jnp.where(h == 0, 16, 9), flat, 0)
        acc = dot3(th[...], tl[...], fh[pl.ds(base, 256), :], fl[pl.ds(base, 256), :], NT)
        sent[2 * q] = acc[:, :128]

        @pl.when(h == 0)
        def _():
            sent[2 * q + 1] = acc[:, 128:]

        @pl.when(h == 1)
        def _():
            for i in range(OWN):
                parts = [jnp.where(narrow, acc[BAND * i + 8 * b:BAND * i + 8 * b + 8, 128:], 0.0) for b in range(10)]
                first = parts[0]
                for b in range(1, 8):
                    first = first + pltpu.roll(parts[b], 16 * b, 1)
                sentl[c2, pl.ds(16 * i, 8), :] = first
                sentl[c2, pl.ds(16 * i + 8, 8), :] = parts[8] + pltpu.roll(parts[9], 16, 1)

        @pl.when(q == 0)
        def _():
            pl.semaphore_wait(barrier, 16 + 7 - jnp.where(src1 == c, 1, 0))

        wd = y * 2 + c2

        def put(src, dst, j, k, tile):
            @pl.when((j != g) | (c2 != c))
            def _():
                pltpu.make_async_remote_copy(
                    src_ref=src, dst_ref=dst, send_sem=s1.at[q, k], recv_sem=r1.at[tile, g],
                    device_id=(wd, j), device_id_type=MESH).start()

            @pl.when((j == g) & (c2 == c))
            def _():
                pltpu.make_async_copy(src, dst, l1).start()
                pltpu.make_async_copy(src, dst, l1).wait()

        def send(k, carry):
            i = lax.rem(k + g, 8)
            e = 1 - k // 8
            j = 8 * c + i
            tile = 2 * h + e

            @pl.when(tile < 3)
            def _():
                put(sent.at[2 * q + e, pl.ds(i * BAND, ROWS), :], got.at[tile, pl.ds(ROWS * g, ROWS), :], j, k, tile)

            @pl.when(tile == 3)
            def _():
                put(sentl.at[c2, pl.ds(16 * i, 16), :], gotl.at[pl.ds(16 * g, 16), :], j, k, tile)
            return carry

        lax.fori_loop(0, 16, send, 0)
        return carry

    lax.fori_loop(0, 4, stage1, 0)

    def pass_on(d, carry):
        @pl.when(d != w)
        def _():
            pl.semaphore_signal(ready, inc=1, device_id=(d, g), device_id_type=MESH)
        return carry

    lax.fori_loop(0, 8, pass_on, 0)

    for n in range(4):
        for v in range(8):
            m[n, pl.ds(128 * v + COLS, 128 - COLS), :] = jnp.zeros((128 - COLS, 128), F32)

    pair = 16 * y + g

    def arrive(*tiles):
        for tile in tiles:
            def one(gs, carry):
                @pl.when((gs != g) | (src1 != c))
                def _():
                    if tile < 3:
                        src, dst = sent.at[0, pl.ds(0, ROWS), :], got.at[tile, pl.ds(ROWS * gs, ROWS), :]
                    else:
                        src, dst = sentl.at[0, pl.ds(0, 16), :], gotl.at[pl.ds(16 * gs, 16), :]
                    pltpu.make_async_remote_copy(
                        src_ref=src, dst_ref=dst, send_sem=s1.at[0, 0], recv_sem=r1.at[tile, gs],
                        device_id=(w, g), device_id_type=MESH).wait_recv()
                return carry

            lax.fori_loop(0, 16, one, 0)

    def multiply(h):
        def halves(b, carry):
            at = pl.multiple_of(b * 128, 128)
            here = lax.broadcasted_iota(jnp.int32, (128, 128), 1)
            for e in range(2):
                n = 2 * h + e
                value = got[n, pl.ds(at, 128), :]
                if n:
                    before = got[n - 1, pl.ds(at, 128), :]
                    value = jnp.where(here < 28 * n, pltpu.roll(before, 28 * n, 1), pltpu.roll(value, 28 * n, 1))
                hi, lo = split(value)
                ah[pl.ds(at, 128), pl.ds(128 * e, 128)] = hi
                al[pl.ds(at, 128), pl.ds(128 * e, 128)] = lo
            return carry

        lax.fori_loop(0, DEPTH // 128, halves, 0, unroll=10)

        def rows_of(half, carry):
            side = lax.rem(half + other, 2)
            at = pl.multiple_of(side * 512, 512)
            mine = pl.ds(pl.multiple_of(side * 400, 16), 400)
            product[...] = dot3(fh[mine, :], fl[mine, :], ah[...], al[...], NN)
            for a in range(4):
                for e in range(2):
                    m[2 * h + e, pl.ds(at + 128 * a, COLS), :] = product[pl.ds(COLS * a, COLS), pl.ds(128 * e, 128)]

            @pl.when(half == 0)
            def _():
                for e in range(2):
                    pltpu.make_async_remote_copy(
                        src_ref=m.at[2 * h + e, pl.ds(at, 512), :], dst_ref=xr.at[2 * h + e],
                        send_sem=sx.at[2 * h + e], recv_sem=rx.at[2 * h + e],
                        device_id=(y * 2 + other, g), device_id_type=MESH).start()
            return carry

        lax.fori_loop(0, 2, rows_of, 0)

    def crossed(h):
        for n in (2 * h, 2 * h + 1):
            pltpu.make_async_remote_copy(
                src_ref=m.at[n, pl.ds(0, 512), :], dst_ref=xr.at[n], send_sem=sx.at[n], recv_sem=rx.at[n],
                device_id=(w, g), device_id_type=MESH).wait()

    main = lax.broadcasted_iota(jnp.int32, (8, 128), 1) < COLS

    def add(across, a, n):
        half = other if across else c
        at = pl.multiple_of((4 * half + a) * 128, 128)
        if across:
            back = xr[a, pl.ds(pl.multiple_of(n * 128, 128), 128), :]
        else:
            back = m[a, pl.ds(pl.multiple_of((4 * c + n) * 128, 128), 128), :]
        whole[...] = m[n, pl.ds(at, 128), :] + back.T
        for r in range(2):
            slot = 2 * (4 * half + a) + r
            rest = whole[pl.ds(KROWS * r + SENT, 8), :]
            for j in range(4):
                n_[n, slot, pl.ds(8 * j, 8), :] = jnp.where(
                    main, whole[pl.ds(KROWS * r + 8 * j, 8), :], pltpu.roll(rest, COLS - 25 * j, 1))
            n_[n, slot, pl.ds(32, SENT - 32), :] = whole[pl.ds(KROWS * r + 32, SENT - 32), :]

    def spread(half, a, n, r):
        v = 4 * half + a
        wd = 4 * c + n
        gd = 2 * v + r
        src = n_.at[n, gd, pl.ds(0, SENT), :]
        dst = o.at[pl.ds(pair * SLOT, SENT), :]

        @pl.when((gd != g) | (wd != w))
        def _():
            pltpu.make_async_remote_copy(
                src_ref=src, dst_ref=dst, send_sem=s2.at[n, gd], recv_sem=r2.at[pair],
                device_id=(wd, gd), device_id_type=MESH).start()

        @pl.when((gd == g) & (wd == w))
        def _():
            pltpu.make_async_copy(src, dst, l2).start()
            pltpu.make_async_copy(src, dst, l2).wait()

    arrive(0, 1)
    multiply(0)
    crossed(0)

    def quarter(t, carry):
        add(False, t // 2, lax.rem(t, 2))
        add(True, t // 2, lax.rem(t, 2))
        return carry

    lax.fori_loop(0, 4, quarter, 0)

    pl.semaphore_wait(ready, 7)
    arrive(3)
    for gs in range(16):
        for b in range(10):
            part = gotl[pl.ds(16 * gs + 8 * (b // 8), 8), :]
            if b % 8:
                part = pltpu.roll(part, 128 - 16 * (b % 8), 1)
            got[3, pl.ds(ROWS * gs + 8 * b, 8), :] = part
    arrive(2)
    multiply(1)
    z, x = g // 4, lax.rem(g, 4)

    def out(t, carry):
        k = lax.rem(t * 11, 64)
        zd = 2 * lax.rem(k // 32 + c, 2) + lax.rem(k // 16 + z, 2)
        xd = lax.rem(k // 4 + x, 4)
        n = lax.rem(k + y, 4)
        half, r = zd // 2, lax.rem(xd, 2)
        a = 2 * lax.rem(zd, 2) + xd // 2
        twin = 16 * (k // 16) + 4 * lax.rem(xd + 1 - 2 * r + 4 - x, 4) + lax.rem(k, 4)
        first = ((a > 1) | (n > 1)) & (t < lax.rem(twin * 35, 64))

        @pl.when(t == 3)
        def _():
            crossed(1)

        @pl.when(first & (half == c))
        def _():
            add(False, a, n)

        @pl.when(first & (half != c))
        def _():
            add(True, a, n)

        spread(half, a, n, r)
        return carry

    lax.fori_loop(0, 64, out, 0)

    def left1(k, carry):
        q, kk = k // 16, lax.rem(k, 16)
        j = 8 * c + lax.rem(kk + g, 8)
        last = (q >= 2) & (kk < 8)
        moved = (j != g) | (lax.rem(q, 2) != c)

        def gone(src):
            pltpu.make_async_remote_copy(
                src_ref=src, dst_ref=src, send_sem=s1.at[q, kk], recv_sem=r1.at[0, 0],
                device_id=(w, g), device_id_type=MESH).wait_send()

        @pl.when(moved & jnp.logical_not(last))
        def _():
            gone(sent.at[0, pl.ds(0, ROWS), :])

        @pl.when(moved & last)
        def _():
            gone(sentl.at[0, pl.ds(0, 16), :])
        return carry

    lax.fori_loop(0, 64, left1, 0)

    def left2(k, carry):
        n, gd = k // 16, lax.rem(k, 16)

        @pl.when((gd != g) | (4 * c + n != w))
        def _():
            pltpu.make_async_remote_copy(
                src_ref=n_.at[0, 0, pl.ds(0, SENT), :], dst_ref=o.at[pl.ds(0, SENT), :],
                send_sem=s2.at[n, gd], recv_sem=r2.at[0], device_id=(w, g), device_id_type=MESH).wait_send()
        return carry

    lax.fori_loop(0, 64, left2, 0)

    def landed(q, carry):
        @pl.when((q != pair) | (src2 != c))
        def _():
            pltpu.make_async_remote_copy(
                src_ref=n_.at[0, 0, pl.ds(0, SENT), :], dst_ref=o.at[pl.ds(q * SLOT, SENT), :],
                send_sem=s2.at[0, 0], recv_sem=r2.at[q], device_id=(w, g), device_id_type=MESH).wait_recv()
        return carry

    lax.fori_loop(0, PAIRS, landed, 0)


def arrange(o_ref, out_ref, ready, sems):
    lane = lax.broadcasted_iota(jnp.int32, (8, 128), 1)

    def plain(k, carry):
        for b in range(PAIRS // 8):
            ready[k, pl.ds(8 * b, 8), :] = o_ref[pl.ds(8 * b * SLOT + k, 8, stride=SLOT), :][:, :COLS]
        return carry

    def parts(q, carry):
        for b in range(PAIRS // 8):
            value = jnp.zeros((8, 128), F32)
            for j in range(4):
                part = o_ref[pl.ds(8 * b * SLOT + 8 * j + q, 8, stride=SLOT), :]
                part = pltpu.roll(part, 28 + 25 * j, 1)
                value = part if j == 0 else jnp.where(lane >= 25 * j, part, value)
            ready[SENT + q, pl.ds(8 * b, 8), :] = value[:, :COLS]
        return carry

    copies = []
    for n, (start, rows) in enumerate(((SENT, 8), (0, 14), (14, 14), (28, 14))):
        if start == SENT:
            lax.fori_loop(0, 8, parts, 0, unroll=2)
        else:
            lax.fori_loop(start, start + rows, plain, 0, unroll=7)
        copies.append(pltpu.make_async_copy(ready.at[pl.ds(start, rows)], out_ref.at[pl.ds(start, rows)], sems.at[n]))
        copies[-1].start()
    for copy in copies:
        copy.wait()


def on_device(integrals, coeffs):
    dma = pltpu.SemaphoreType.DMA
    blocks = pl.pallas_call(
        kernel,
        out_shape=jax.ShapeDtypeStruct(((PAIRS + 1) * SLOT, 128), F32),
        in_specs=[pl.BlockSpec(memory_space=pl.ANY)] * 2,
        out_specs=pl.BlockSpec(memory_space=pl.ANY),
        scratch_shapes=[
            pltpu.VMEM((OWN, ROWS, NAO), F32),
            pltpu.VMEM((800, NAO), F32),
            pltpu.VMEM((OWN * BAND, DEPTH), BF16),
            pltpu.VMEM((OWN * BAND, DEPTH), BF16),
            pltpu.VMEM((912, DEPTH), BF16),
            pltpu.VMEM((912, DEPTH), BF16),
            pltpu.VMEM((8, OWN * BAND, 128), F32),
            pltpu.VMEM((2, OWN * 16, 128), F32),
            pltpu.VMEM((4, DEPTH, 128), F32),
            pltpu.VMEM((256, 128), F32),
            pltpu.VMEM((DEPTH, 256), BF16),
            pltpu.VMEM((DEPTH, 256), BF16),
            pltpu.VMEM((400, 256), F32),
            pltpu.VMEM((4, 1024, 128), F32),
            pltpu.VMEM((4, 512, 128), F32),
            pltpu.VMEM((128, 128), F32),
            pltpu.VMEM((4, 16, SLOT, 128), F32),
            dma((OWN,)), dma,
            dma((4, 16)), dma((4, 16)), dma,
            dma((4,)), dma((4,)),
            dma((4, 16)), dma((PAIRS,)), dma, pltpu.SemaphoreType.REGULAR,
        ],
        compiler_params=pltpu.CompilerParams(
            collective_id=0, has_side_effects=True, vmem_limit_bytes=51 * 2**20),
    )(integrals, coeffs.T)
    slab = pl.pallas_call(
        arrange,
        out_shape=jax.ShapeDtypeStruct((KROWS, PAIRS, COLS), F32),
        in_specs=[pl.BlockSpec(memory_space=pltpu.VMEM)],
        out_specs=pl.BlockSpec(memory_space=pl.ANY),
        scratch_shapes=[pltpu.VMEM((KROWS, PAIRS, COLS), F32), dma((4,))],
        compiler_params=pltpu.CompilerParams(vmem_limit_bytes=16 * 2**20),
    )(blocks)
    return jnp.transpose(slab, (0, 2, 1))


def solution(mesh):
    return jax.shard_map(
        on_device,
        mesh=mesh,
        in_specs=(P("grp", "wide", None), P()),
        out_specs=P("grp", "wide", None),
        check_vma=False,
    )
```
